256 devices in a mesh: rep: 32 (over x, z), shard: 8 (over y, core).
Axes of the slice: x: 4, y: 4, z: 8, core: 2. Of those that a mesh axis runs over, the one named last changes fastest.
Arguments:
- gradient: bfloat16 [32, 2, 3072, 3072], P('rep', None, 'shard')
- error_buffer: bfloat16 [32, 2, 3072, 3072], P('rep', None, 'shard'), may hold values from -4 to 4
- previous_q: float32 [2, 3072, 32], replicated, may hold values from -0.109375 to 0.109375
- run_starts: int32 [32], replicated, may hold values from 0 to 2952, as said below
- run_owners: int32 [32], replicated, may hold values from 0 to 7, as said below
Outputs:
- left_factor: float32 [2, 3072, 32], P(None, 'shard')
- right_factor: float32 [2, 3072, 32], replicated
The draws below stay inside these ranges and needn't reach their ends.
Inputs may be any that keep to these rules, and one draw needn't show every extreme that they name: `run_starts`: Rising; the runs of device i's flat shard of rows are entries 4 * i to 4 * i + 3, the first starting at row i * 384; every run is a positive multiple of 24 rows long, and every shard is cut into the same four run lengths in some order, one of them 120 rows; the last run is 120 rows long. `run_owners`: the four runs of one shard go to four different owners; every owner receives 384 rows in all and at most 120 rows from one shard.
All inputs are finite; a program needn't handle non-finite values.
Results may differ from the reference program's by a relative error of at most 0.0045.
Values sent between devices are 32-bit elements; how exact they have to be, the bound alone decides.
No kernel may reach another device: no remote copies, remote signals or barrier semaphores. Data moves between devices by JAX's collectives and lax.ppermute only.
A program may use at most 64 MiB of HBM per device.

```python
import math
import jax
import jax.numpy as jnp
from jax import lax

MROWS = 3072
MCOLS = 3072
RANK = 32
LAYERS = 2
REPLICAS = 32
N_SHARD = 8


def run_layout(key):
    keys = jax.random.split(key, 6)
    count = N_SHARD
    granule = MROWS // N_SHARD // 16
    first_extra = jax.random.randint(keys[0], (), 1, 6)
    second_extra = jax.random.randint(keys[1], (), jnp.maximum(1, 6 - first_extra), jnp.minimum(5, 10 - first_extra) + 1)
    third_extra = 11 - first_extra - second_extra
    amounts = jnp.stack([jnp.array(5, jnp.int32), first_extra.astype(jnp.int32), second_extra.astype(jnp.int32), third_extra.astype(jnp.int32)])
    amounts = jax.random.permutation(keys[2], amounts)
    shifts = jax.random.permutation(keys[3], count).astype(jnp.int32)
    labels = jax.random.permutation(keys[4], count).astype(jnp.int32)
    slots = jnp.arange(4, dtype=jnp.int32)
    run_owner = labels[(shifts[:, None] + slots[None, :]) % count]
    orders = jax.vmap(lambda sub_key: jax.random.permutation(sub_key, 4))(jax.random.split(keys[5], count)).astype(jnp.int32)
    lengths = amounts[orders] * granule
    owners = jnp.take_along_axis(run_owner, orders, axis=1)
    last_order = jnp.argsort(lengths[count - 1], stable=True)
    lengths = lengths.at[count - 1].set(lengths[count - 1][last_order])
    owners = owners.at[count - 1].set(owners[count - 1][last_order])
    starts = jnp.arange(count, dtype=jnp.int32)[:, None] * (MROWS // N_SHARD) + jnp.cumsum(lengths, axis=1) - lengths
    return (starts.reshape(-1).astype(jnp.int32), owners.reshape(-1).astype(jnp.int32))


def draw_run_starts(key, part):
    starts, owners = run_layout(key)
    return starts


def draw_run_owners(key, part):
    starts, owners = run_layout(key)
    return owners


def draw_gradient(key, part):
    key = jax.random.fold_in(key, 11)
    keys = jax.random.split(key, 3)
    shape = (REPLICAS, LAYERS, MROWS, MCOLS)
    position = jnp.arange(MROWS, dtype=jnp.float32) / MROWS
    row_scale = jnp.exp(jax.random.uniform(keys[1], (REPLICAS, LAYERS, MROWS, 1)) * jnp.log(10.0)) * 0.3
    col_scale = jnp.exp(jax.random.uniform(keys[2], (1, 1, 1, MCOLS)) * jnp.log(10.0)) * 0.3
    ramp = (3.0 ** (0.5 * position))[None, None, :, None]
    values = jax.random.normal(keys[0], shape) * row_scale * col_scale * ramp
    return values.astype(jnp.bfloat16)


def steps_of(stream_key, extent, cuts, smallest, high):
    level, own = 1.0, jax.random.fold_in(stream_key, 6)
    for axis_at, parts in cuts:
        heights = jnp.exp(jax.random.uniform(jax.random.fold_in(own, axis_at), (parts,), jnp.float32, smallest / len(cuts), high / len(cuts)))
        level = level * jnp.repeat(heights, extent[axis_at] // parts).reshape([-1 if axis == axis_at else 1 for axis in range(len(extent))])
    return level


def centred(own_key, dims, scale, most, shards=(), kind=jnp.bfloat16):
    result = jax.random.normal(own_key, dims, jnp.float32) * scale
    if len(shards) > 0:
        result = steps_of(own_key, dims, shards, -0.22, 0.18) * result
    return jnp.clip(result, min=-most, max=most).astype(kind)


def setup_inputs(seed: int = 0) -> dict:
    key_of = jax.random.split(jax.random.key(seed), 6)
    return {
        "gradient": draw_gradient(jax.random.fold_in(key_of[5], 71), 0),
        "error_buffer": centred(key_of[1], (REPLICAS, LAYERS, MROWS, MCOLS), 0.5, 4.0, ((0, 32), (2, 8))),
        "previous_q": centred(key_of[2], (LAYERS, MCOLS, RANK), MCOLS ** -0.5, 0.109375, (), jnp.float32),
        "run_starts": draw_run_starts(jax.random.fold_in(key_of[5], 71), 0),
        "run_owners": draw_run_owners(jax.random.fold_in(key_of[5], 71), 0),
    }


def row_owners(run_starts, run_owners, total_rows):
    positions = jnp.arange(total_rows, dtype=jnp.int32)
    run_ends = jnp.concatenate([run_starts[1:], jnp.full((1,), total_rows, jnp.int32)])
    inside = (run_starts[None, :] <= positions[:, None]) & (positions[:, None] < run_ends[None, :])
    return lax.optimization_barrier(jnp.sum(jnp.where(inside, run_owners[None, :], 0), axis=1)).astype(jnp.int32)

def orthonormal(factor, gram_matrix):
    cholesky_factor = jnp.linalg.cholesky(gram_matrix)

    def solve_one(triangle, right_side):
        return jax.scipy.linalg.solve_triangular(triangle, right_side, lower=True)
    solved = jax.vmap(solve_one)(cholesky_factor, jnp.swapaxes(factor, 1, 2))
    return jnp.swapaxes(solved, 1, 2)

def reference(gradient, error_buffer, previous_q, run_starts, run_owners):
    q_low = previous_q.astype(jnp.bfloat16)

    def merged_of(replica):
        return (gradient[replica].astype(jnp.float32) + error_buffer[replica].astype(jnp.float32)).astype(jnp.bfloat16)

    def add_left(total, replica):
        merged = merged_of(replica)
        terms = jnp.stack([jnp.dot(merged[layer_index].astype(jnp.float32), q_low[layer_index].astype(jnp.float32), preferred_element_type=jnp.float32) for layer_index in range(LAYERS)])
        return (total + terms, None)
    factor_sum, unused = lax.scan(add_left, jnp.zeros((LAYERS, MROWS, RANK), jnp.float32), jnp.arange(REPLICAS))
    gram_matrix = jnp.einsum('lrk,lrj->lkj', factor_sum, factor_sum, precision=lax.Precision.HIGHEST)
    basis = orthonormal(factor_sum, gram_matrix)
    basis_low = basis.astype(jnp.bfloat16)

    def add_right(total, replica):
        merged = merged_of(replica)
        terms = jnp.stack([jnp.dot(merged[layer_index].T.astype(jnp.float32), basis_low[layer_index].astype(jnp.float32), preferred_element_type=jnp.float32) for layer_index in range(LAYERS)])
        return (total + terms, None)
    right_factor, unused = lax.scan(add_right, jnp.zeros((LAYERS, MCOLS, RANK), jnp.float32), jnp.arange(REPLICAS))
    owners = row_owners(run_starts, run_owners, MROWS)
    ordering = jnp.argsort(owners * MROWS + jnp.arange(MROWS, dtype=jnp.int32))
    left_factor = (basis * math.sqrt(MROWS))[:, ordering, :]
    return (left_factor, right_factor)
```

```python
import functools
import math

import jax
import jax.numpy as jnp
from jax import lax
from jax.experimental import pallas as pl
from jax.experimental.pallas import tpu as pltpu
from jax.sharding import PartitionSpec as P

LAYERS = 2
RANK = 32
ROWS = 384
COLS = 3072
HALF = COLS // 2
REP = 32
YS = 4
BLOCKS = ROWS // 128
ROW_TILES = LAYERS * RANK // 8
TILES = ROW_TILES * BLOCKS
LEFT, GRAM, SCALE, SLOTS = TILES, TILES + 1, TILES + 3, TILES + 4
VMEM_LIMIT = 40 * 1024 * 1024
F32 = jnp.float32
BF16 = jnp.bfloat16


def whole(memory_space=pltpu.VMEM):
    return pl.BlockSpec(memory_space=memory_space)


def params(**more):
    return pltpu.CompilerParams(vmem_limit_bytes=VMEM_LIMIT, **more)


def split3(value):
    high = value.astype(BF16)
    rest = value - high.astype(F32)
    middle = rest.astype(BF16)
    low = (rest - middle.astype(F32)).astype(BF16)
    return high, middle, low


def dot_rows(left, right):
    return lax.dot_general(left, right, (((1,), (1,)), ((), ())), preferred_element_type=F32)


def merge_kernel(gradient, error, q, merged, partial):
    layer, block = pl.program_id(0), pl.program_id(1)
    total = (gradient[0, 0].astype(F32) + error[0, 0].astype(F32)).astype(BF16)
    merged[0] = total
    terms = dot_rows(q[0].astype(BF16), total)
    for part in range(RANK // 8):
        partial[(layer * (RANK // 8) + part) * BLOCKS + block] = terms[part * 8 : part * 8 + 8]

    @pl.when((layer == 0) & (block == 0))
    def _():
        partial[TILES:] = jnp.zeros((REP - TILES, 8, 128), F32)


def merge(gradient, error, q):
    block = pl.BlockSpec((1, 1, 128, COLS), lambda l, b: (0, l, b, 0))
    return pl.pallas_call(
        merge_kernel,
        grid=(LAYERS, BLOCKS),
        in_specs=[block, block, pl.BlockSpec((1, RANK, COLS), lambda l, b: (l, 0, 0))],
        out_specs=[
            pl.BlockSpec((1, 128, COLS), lambda l, b: (l, b, 0)),
            pl.BlockSpec((REP, 8, 128), lambda l, b: (0, 0, 0)),
        ],
        out_shape=[
            jax.ShapeDtypeStruct((LAYERS, ROWS, COLS), BF16),
            jax.ShapeDtypeStruct((REP, 8, 128), F32),
        ],
        compiler_params=params(),
        name="merge_project",
    )(gradient, error, q)


def rows_of(tiles):
    return jnp.concatenate(
        [
            jnp.concatenate([tiles[row * BLOCKS + block] for block in range(BLOCKS)], axis=1)
            for row in range(ROW_TILES)
        ],
        axis=0,
    )


def product_kernel(with_extras, place, dest, tiles, merged, out):
    rep, half = place[0], place[3]
    factor = rows_of(tiles)
    biggest = [
        jnp.max(jnp.abs(factor[l * RANK : l * RANK + RANK]), keepdims=True) for l in range(LAYERS)
    ]
    scales = [jnp.where(b > 0, b * 64.0, 1.0) for b in biggest]
    for layer in range(LAYERS):
        scaled = factor[layer * RANK : layer * RANK + RANK] * (1.0 / scales[layer])
        parts = jnp.concatenate(split3(scaled), axis=0)
        for y in range(YS):
            first = pl.multiple_of(half * HALF + y * ROWS, 128)
            product = jnp.dot(
                parts, merged[layer, :, pl.ds(first, ROWS)], preferred_element_type=F32
            )
            product = product[:RANK] + product[RANK : 2 * RANK] + product[2 * RANK :]
            for part in range(RANK // 8):
                for block in range(BLOCKS):
                    out[y, (layer * (RANK // 8) + part) * BLOCKS + block] = product[
                        part * 8 : part * 8 + 8, block * 128 : block * 128 + 128
                    ]
    tile = jnp.minimum(rep, TILES - 1)
    row_tile = tile // BLOCKS
    column = (tile - row_tile * BLOCKS) * 128
    rows = jnp.concatenate([tiles[row_tile * BLOCKS + block] for block in range(BLOCKS)], axis=1)
    rows = jnp.concatenate(split3(rows), axis=0)
    wanted = jnp.broadcast_to(dest[0:1], (128, ROWS)) - lax.broadcasted_iota(
        jnp.int32, (128, ROWS), 0
    )
    for y in range(YS):
        base = (y * 2 + half) * ROWS + column
        chosen = jnp.where(wanted == base, 1.0, 0.0).astype(BF16)
        found = dot_rows(rows, chosen)
        out[y, LEFT] = found[:8] + found[8:16] + found[16:]
    high, middle, low = split3(factor)
    left = jnp.concatenate([high, middle, low], axis=0)
    right = jnp.concatenate([high, high, middle, middle, low, low], axis=0)
    gram = dot_rows(left, right)
    gram = gram[:64] + gram[64:128] + gram[128:]
    gram = gram[:, :128] + gram[:, 128:256] + gram[:, 256:]
    lane = lax.broadcasted_iota(jnp.int32, (RANK, 128), 1)
    gram = jnp.where(lax.rem(lane, 64) < 32, gram[:RANK], gram[RANK:])
    gram = jnp.where(lane[:16] < 64, gram[:16], gram[16:])
    scale = jnp.concatenate([jnp.broadcast_to(s, (4, 128)) for s in scales], axis=0)
    for y in range(YS):
        out[y, GRAM] = gram[:8]
        out[y, GRAM + 1] = gram[8:]
        out[y, SCALE] = scale


def product(place, dest, tiles, merged, name):
    return pl.pallas_call(
        functools.partial(product_kernel, True),
        in_specs=[whole(pltpu.SMEM), whole(), whole(), whole()],
        out_specs=whole(),
        out_shape=jax.ShapeDtypeStruct((YS, SLOTS, 8, 128), F32),
        compiler_params=params(),
        name=name,
    )(place, dest, tiles, merged)


def add_scaled(pieces):
    largest = functools.reduce(jnp.maximum, [p[SCALE] for p in pieces])
    ratios = [p[SCALE] / largest for p in pieces]
    out = []
    for slot in range(SLOTS):
        if slot == SCALE:
            out.append(largest)
        elif slot < TILES:
            row = 0 if slot < TILES // 2 else 4
            out.append(
                functools.reduce(
                    jnp.add, [p[slot] * r[row : row + 1] for p, r in zip(pieces, ratios)]
                )
            )
        else:
            out.append(functools.reduce(jnp.add, [p[slot] for p in pieces]))
    return out


def pair_kernel(mine, other, out):
    for y in range(YS):
        summed = add_scaled([[ref[y, s] for s in range(SLOTS)] for ref in (mine, other)])
        for slot in range(SLOTS):
            out[y, slot] = summed[slot]


def pair(mine, other):
    return pl.pallas_call(
        pair_kernel,
        in_specs=[whole(), whole()],
        out_specs=whole(),
        out_shape=jax.ShapeDtypeStruct((YS, SLOTS, 8, 128), F32),
        compiler_params=params(),
        name="add_cores",
    )(mine, other)


def line_kernel(pieces, product_out, rest_out):
    summed = add_scaled([[pieces[y, s] for s in range(SLOTS)] for y in range(YS)])
    for slot in range(TILES):
        product_out[slot] = summed[slot]
    product_out[TILES:] = jnp.zeros((REP - TILES, 8, 128), F32)
    for slot in range(TILES, SLOTS):
        rest_out[slot - TILES] = summed[slot]


def line(pieces):
    return pl.pallas_call(
        line_kernel,
        in_specs=[whole()],
        out_specs=[whole(), whole()],
        out_shape=[
            jax.ShapeDtypeStruct((REP, 8, 128), F32),
            jax.ShapeDtypeStruct((SLOTS - TILES, 8, 128), F32),
        ],
        compiler_params=params(),
        name="add_line",
    )(pieces)


def invert_kernel(rest, out):
    packed = jnp.concatenate([rest[GRAM - LEFT], rest[GRAM + 1 - LEFT]], axis=0)
    turned = pltpu.roll(packed, 64, 1)
    row = lax.broadcasted_iota(jnp.int32, (RANK, 128), 0)
    lane = lax.broadcasted_iota(jnp.int32, (RANK, 128), 1)
    gram = jnp.concatenate([packed, turned], axis=0)
    unit = jnp.where(row == lax.rem(lane, RANK), 1.0, 0.0)
    work = jnp.where(lane < 64, gram, unit)
    first = lax.rem(lane, 64) < RANK
    for step in range(RANK - 1):
        column = jnp.where(
            first,
            jnp.broadcast_to(work[:, step : step + 1], (RANK, 128)),
            jnp.broadcast_to(work[:, RANK + step : RANK + step + 1], (RANK, 128)),
        )
        pivot = work[step : step + 1] / column[step : step + 1]
        work = work - jnp.where(row > step, column, 0.0) * pivot
    diagonal = [
        jnp.sum(jnp.where(lane == row + l * RANK, work, 0.0), axis=1, keepdims=True)
        for l in range(LAYERS)
    ]
    root = jnp.where(
        first,
        jnp.broadcast_to(diagonal[0], (RANK, 128)),
        jnp.broadcast_to(diagonal[1], (RANK, 128)),
    )
    inverse = pltpu.roll(work / jnp.sqrt(root), 64, 1)
    left = jnp.concatenate(
        [jnp.where(lane < RANK, inverse, 0.0), jnp.where((lane >= RANK) & (lane < 64), inverse, 0.0)],
        axis=0,
    )
    scale = rest[SCALE - LEFT]
    out[0] = left * math.sqrt(COLS)
    out[1] = jnp.concatenate(
        [left[:RANK] * scale[0:1], left[RANK:] * scale[4:5]], axis=0
    )


def invert(rest):
    return pl.pallas_call(
        invert_kernel,
        in_specs=[whole()],
        out_specs=whole(),
        out_shape=jax.ShapeDtypeStruct((2, 64, 128), F32),
        compiler_params=params(),
        cost_estimate=pl.CostEstimate(flops=2_000_000, bytes_accessed=20_000_000, transcendentals=0),
        name="invert_triangle",
    )(rest)


def finish_kernel(tiles, inverse, left_out, right_out):
    for which, out in ((1, None), (0, left_out)):
        rows = rows_of([tiles[t, 1 - which] for t in range(TILES)])
        done = jnp.dot(
            inverse[which][:, :64],
            rows,
            precision=lax.Precision.HIGHEST,
            preferred_element_type=F32,
        )
        if out is not None:
            out[0] = done[:RANK]
            out[1] = done[RANK:]
        else:
            for t in range(TILES):
                row, block = divmod(t, BLOCKS)
                tile = done[row * 8 : row * 8 + 8, block * 128 : block * 128 + 128]
                for y in range(YS):
                    right_out[y, t] = tile


def finish(tiles, inverse):
    return pl.pallas_call(
        finish_kernel,
        in_specs=[whole(), whole()],
        out_specs=[whole(), whole()],
        out_shape=[
            jax.ShapeDtypeStruct((LAYERS, RANK, ROWS), F32),
            jax.ShapeDtypeStruct((YS, TILES, 8, 128), F32),
        ],
        compiler_params=params(),
        name="apply_triangle",
    )(tiles, inverse)


def assemble_kernel(place, mine, other, out):
    for ref, half in ((mine, place[2]), (other, 1 - place[2])):
        for y in range(YS):
            for t in range(TILES):
                row, block = divmod(t, BLOCKS)
                layer, row = divmod(row, RANK // 8)
                first = pl.multiple_of(half * HALF + y * ROWS + block * 128, 128)
                out[layer, row * 8 : row * 8 + 8, pl.ds(first, 128)] = ref[y, t]


def assemble(place, mine, other):
    return pl.pallas_call(
        assemble_kernel,
        in_specs=[whole(pltpu.SMEM), whole(), whole()],
        out_specs=whole(),
        out_shape=jax.ShapeDtypeStruct((LAYERS, RANK, COLS), F32),
        compiler_params=params(),
        name="assemble_right",
    )(place, mine, other)


def sum_kernel(pieces, *refs):
    out = refs[-1]
    total = functools.reduce(jnp.add, [pieces[r] for r in range(REP)])
    if len(refs) == 1:
        for r in range(REP):
            out[r] = total
    else:
        rest = refs[0]
        for r in range(REP):
            out[r, 0] = total
            out[r, 1] = rest[0]


def sum_and_copy(pieces, rest=None):
    shape = (REP, 8, 128) if rest is None else (REP, 2, 8, 128)
    operands = (pieces,) if rest is None else (pieces, rest)
    return pl.pallas_call(
        sum_kernel,
        in_specs=[whole()] * len(operands),
        out_specs=whole(),
        out_shape=jax.ShapeDtypeStruct(shape, F32),
        compiler_params=params(),
        name="add_replicas",
    )(*operands)


def destinations(run_starts, run_owners, shard):
    ends = jnp.concatenate([run_starts[1:], jnp.full((1,), COLS, jnp.int32)])
    lengths = ends - run_starts
    index = jnp.arange(REP, dtype=jnp.int32)
    before = (index[None, :] < index[:, None]) & (run_owners[None, :] == run_owners[:, None])
    offset = jnp.sum(jnp.where(before, lengths[None, :], 0), axis=1)
    shift = run_owners * ROWS + offset - run_starts
    position = shard * ROWS + jnp.arange(ROWS, dtype=jnp.int32)
    inside = (run_starts[:, None] <= position[None, :]) & (position[None, :] < ends[:, None])
    row = position + jnp.sum(jnp.where(inside, shift[:, None], 0), axis=0)
    return jnp.broadcast_to(row[None, :], (8, ROWS))


def exchange(value, axis):
    return lax.all_to_all(value, axis, split_axis=0, concat_axis=0, tiled=True)


def swap(value):
    return lax.ppermute(value, "core", [(0, 1), (1, 0)])


def shards(gradient, error_buffer, previous_q, run_starts, run_owners):
    rep = lax.axis_index("x") * 8 + lax.axis_index("z")
    line_at, core = lax.axis_index("y"), lax.axis_index("core")
    dest = destinations(run_starts, run_owners, line_at * 2 + core)
    merged, partial = merge(gradient, error_buffer, jnp.swapaxes(previous_q, 1, 2))
    partial = exchange(partial, ("x", "z"))
    tiles = exchange(sum_and_copy(partial), ("x", "z"))
    theirs = jnp.stack([rep, line_at, core, 1 - core]).astype(jnp.int32)
    ours = jnp.stack([rep, line_at, core, core]).astype(jnp.int32)
    sent = swap(product(theirs, dest, tiles, merged, "product_other_half"))
    kept = product(ours, dest, tiles, merged, "product_own_half")
    pieces = exchange(pair(kept, sent), "y")
    terms, rest = line(pieces)
    inverse = invert(rest)
    summed = sum_and_copy(exchange(terms, ("x", "z")), rest)
    left, right = finish(exchange(summed, ("x", "z")), inverse)
    right = exchange(right, "y")
    right = assemble(ours, right, swap(right))
    return (jnp.swapaxes(left, 1, 2), jnp.swapaxes(right, 1, 2))


def solution(mesh):
    grid = jax.sharding.Mesh(mesh.devices.reshape(4, 8, YS, 2), ("x", "z", "y", "core"))
    rep, shard = ("x", "z"), ("y", "core")
    return jax.shard_map(
        shards,
        mesh=grid,
        in_specs=(P(rep, None, shard, None), P(rep, None, shard, None), P(), P(), P()),
        out_specs=(P(None, shard, None), P()),
        check_vma=False,
    )
```

```python
import functools
import math

import jax
import jax.numpy as jnp
from jax import lax
from jax.experimental import pallas as pl
from jax.experimental.pallas import tpu as pltpu
from jax.sharding import PartitionSpec as P

LAYERS = 2
RANK = 32
ROWS = 384
COLS = 3072
HALF = COLS // 2
REP = 32
YS = 4
BLOCKS = ROWS // 128
ROW_TILES = LAYERS * RANK // 8
TILES = ROW_TILES * BLOCKS
LEFT, GRAM, SCALE, SLOTS = TILES, TILES + 1, TILES + 3, TILES + 4
CHUNK = 512
CHUNKS = COLS // CHUNK
RUNS = 4
VMEM_LIMIT = 24 * 1024 * 1024
F32 = jnp.float32
BF16 = jnp.bfloat16


def whole(memory_space=pltpu.VMEM):
    return pl.BlockSpec(memory_space=memory_space)


def params(**more):
    return pltpu.CompilerParams(vmem_limit_bytes=VMEM_LIMIT, **more)


def split3(value):
    high = value.astype(BF16)
    rest = value - high.astype(F32)
    middle = rest.astype(BF16)
    low = (rest - middle.astype(F32)).astype(BF16)
    return high, middle, low


def dot_rows(left, right):
    return lax.dot_general(left, right, (((1,), (1,)), ((), ())), preferred_element_type=F32)


def merge_kernel(
    gradient, error, q, starts, owners, merged, partial, dest, g, e, q_in, table, sems, table_sems
):
    tables = [
        pltpu.make_async_copy(source, table.at[i], table_sems.at[i])
        for i, source in enumerate((starts, owners))
    ]
    for copy in tables:
        copy.start()
    copies = []
    for layer in range(LAYERS):
        copies.append([pltpu.make_async_copy(q.at[layer], q_in.at[layer], sems.at[layer, CHUNKS, 0])])
        for chunk in range(CHUNKS):
            columns = pl.ds(chunk * CHUNK, CHUNK)
            copies.append(
                [
                    pltpu.make_async_copy(
                        source.at[0, layer, :, columns],
                        into.at[layer, chunk],
                        sems.at[layer, chunk, i],
                    )
                    for i, (source, into) in enumerate(((gradient, g), (error, e)))
                ]
            )
    for group in copies:
        for copy in group:
            copy.start()
    partial[TILES:] = jnp.zeros((REP - TILES, 8, 128), F32)
    for copy in tables:
        copy.wait()
    dest[...] = destinations(table)
    arrived = iter(copies)
    for layer in range(LAYERS):
        for copy in next(arrived):
            copy.wait()
        terms = jnp.zeros((RANK, ROWS), F32)
        for chunk in range(CHUNKS):
            for copy in next(arrived):
                copy.wait()
            total = (g[layer, chunk].astype(F32) + e[layer, chunk].astype(F32)).astype(BF16)
            columns = slice(chunk * CHUNK, chunk * CHUNK + CHUNK)
            merged[layer, :, columns] = total
            terms = terms + dot_rows(q_in[layer, :, columns].astype(BF16), total)
        for part in range(RANK // 8):
            for block in range(BLOCKS):
                partial[(layer * (RANK // 8) + part) * BLOCKS + block] = terms[
                    part * 8 : part * 8 + 8, block * 128 : block * 128 + 128
                ]


def destinations(table):
    shard = lax.axis_index("y") * 2 + lax.axis_index("core")
    first = shard * RUNS
    mine = [table[1, first + t] for t in range(RUNS)]

    def count(run, before):
        length = table[0, run + 1] - table[0, run]
        return tuple(b + jnp.where(table[1, run] == o, length, 0) for b, o in zip(before, mine))

    before = lax.fori_loop(0, first, count, (jnp.int32(0),) * RUNS)
    position = shard * ROWS + lax.broadcasted_iota(jnp.int32, (8, ROWS), 1)
    place = position
    for t in range(RUNS):
        start = table[0, first + t]
        moved = position + (mine[t] * ROWS + before[t] - start)
        place = jnp.where(position >= start, moved, place)
    return place


def merge(gradient, error, q, run_starts, run_owners):
    operands = [
        pltpu.with_memory_space_constraint(value, pltpu.HBM)
        for value in (gradient, error, q, run_starts, run_owners)
    ]
    return pl.pallas_call(
        merge_kernel,
        in_specs=[whole(pltpu.HBM)] * 5,
        out_specs=[whole()] * 3,
        out_shape=[
            pltpu.VMEM((LAYERS, ROWS, COLS), BF16),
            jax.ShapeDtypeStruct((REP, 8, 128), F32),
            jax.ShapeDtypeStruct((8, ROWS), jnp.int32),
        ],
        scratch_shapes=[
            pltpu.VMEM((LAYERS, CHUNKS, ROWS, CHUNK), BF16),
            pltpu.VMEM((LAYERS, CHUNKS, ROWS, CHUNK), BF16),
            pltpu.VMEM((LAYERS, RANK, COLS), F32),
            pltpu.SMEM((2, REP), jnp.int32),
            pltpu.SemaphoreType.DMA((LAYERS, CHUNKS + 1, 2)),
            pltpu.SemaphoreType.DMA((2,)),
        ],
        compiler_params=params(),
        name="merge_project",
    )(*operands)


def rows_of(tiles):
    return jnp.concatenate(
        [
            jnp.concatenate([tiles[row * BLOCKS + block] for block in range(BLOCKS)], axis=1)
            for row in range(ROW_TILES)
        ],
        axis=0,
    )


def product_kernel(own, dest, tiles, merged, out):
    rep = lax.axis_index("x") * 8 + lax.axis_index("z")
    half = lax.axis_index("core") if own else 1 - lax.axis_index("core")
    factor = rows_of(tiles)
    biggest = [
        jnp.max(jnp.abs(factor[l * RANK : l * RANK + RANK]), keepdims=True) for l in range(LAYERS)
    ]
    scales = [jnp.where(b > 0, b * 64.0, 1.0) for b in biggest]
    columns = pl.ds(pl.multiple_of(half * HALF, 128), HALF)
    for layer in range(LAYERS):
        scaled = factor[layer * RANK : layer * RANK + RANK] * (1.0 / scales[layer])
        parts = jnp.concatenate(split3(scaled), axis=0)
        product = jnp.dot(parts, merged[layer, :, columns], preferred_element_type=F32)
        product = product[:RANK] + product[RANK : 2 * RANK] + product[2 * RANK :]
        for y in range(YS):
            for part in range(RANK // 8):
                for block in range(BLOCKS):
                    first = y * ROWS + block * 128
                    out[y, (layer * (RANK // 8) + part) * BLOCKS + block] = product[
                        part * 8 : part * 8 + 8, first : first + 128
                    ]
    tile = jnp.minimum(rep, TILES - 1)
    row_tile = tile // BLOCKS
    column = (tile - row_tile * BLOCKS) * 128
    rows = jnp.concatenate([tiles[row_tile * BLOCKS + block] for block in range(BLOCKS)], axis=1)
    rows = jnp.concatenate(split3(rows), axis=0)
    wanted = jnp.broadcast_to(dest[0:1], (128, ROWS)) - lax.broadcasted_iota(
        jnp.int32, (128, ROWS), 0
    )
    for y in range(YS):
        base = (y * 2 + half) * ROWS + column
        chosen = jnp.where(wanted == base, 1.0, 0.0).astype(BF16)
        found = dot_rows(rows, chosen)
        out[y, LEFT] = found[:8] + found[8:16] + found[16:]
    high, middle, low = split3(factor)
    left = jnp.concatenate([high, middle, low], axis=0)
    right = jnp.concatenate([high, high, middle, middle, low, low], axis=0)
    gram = dot_rows(left, right)
    gram = gram[:64] + gram[64:128] + gram[128:]
    gram = gram[:, :128] + gram[:, 128:256] + gram[:, 256:]
    lane = lax.broadcasted_iota(jnp.int32, (RANK, 128), 1)
    gram = jnp.where(lax.rem(lane, 64) < 32, gram[:RANK], gram[RANK:])
    gram = jnp.where(lane[:16] < 64, gram[:16], gram[16:])
    scale = jnp.concatenate([jnp.broadcast_to(s, (4, 128)) for s in scales], axis=0)
    for y in range(YS):
        out[y, GRAM] = gram[:8]
        out[y, GRAM + 1] = gram[8:]
        out[y, SCALE] = scale


def product(own, dest, tiles, merged):
    return pl.pallas_call(
        functools.partial(product_kernel, own),
        in_specs=[whole()] * 3,
        out_specs=whole(),
        out_shape=jax.ShapeDtypeStruct((YS, SLOTS, 8, 128), F32),
        compiler_params=params(),
        name="product_own_half" if own else "product_other_half",
    )(dest, tiles, pltpu.with_memory_space_constraint(merged, pltpu.VMEM))


def add_scaled(pieces):
    largest = functools.reduce(jnp.maximum, [p[SCALE] for p in pieces])
    ratios = [p[SCALE] / largest for p in pieces]
    out = []
    for slot in range(SLOTS):
        if slot == SCALE:
            out.append(largest)
        elif slot < TILES:
            row = 0 if slot < TILES // 2 else 4
            out.append(
                functools.reduce(
                    jnp.add, [p[slot] * r[row : row + 1] for p, r in zip(pieces, ratios)]
                )
            )
        else:
            out.append(functools.reduce(jnp.add, [p[slot] for p in pieces]))
    return out


def pair_kernel(mine, other, out):
    for y in range(YS):
        summed = add_scaled([[ref[y, s] for s in range(SLOTS)] for ref in (mine, other)])
        for slot in range(SLOTS):
            out[y, slot] = summed[slot]


def pair(mine, other):
    return pl.pallas_call(
        pair_kernel,
        in_specs=[whole(), whole()],
        out_specs=whole(),
        out_shape=jax.ShapeDtypeStruct((YS, SLOTS, 8, 128), F32),
        compiler_params=params(),
        name="add_cores",
    )(mine, other)


def line_kernel(pieces, product_out, rest_out):
    summed = add_scaled([[pieces[y, s] for s in range(SLOTS)] for y in range(YS)])
    for slot in range(TILES):
        product_out[slot] = summed[slot]
    product_out[TILES:] = jnp.zeros((REP - TILES, 8, 128), F32)
    for slot in range(TILES, SLOTS):
        rest_out[slot - TILES] = summed[slot]


def line(pieces):
    return pl.pallas_call(
        line_kernel,
        in_specs=[whole()],
        out_specs=[whole(), whole()],
        out_shape=[
            jax.ShapeDtypeStruct((REP, 8, 128), F32),
            jax.ShapeDtypeStruct((SLOTS - TILES, 8, 128), F32),
        ],
        compiler_params=params(),
        name="add_line",
    )(pieces)


def invert_kernel(rest, out):
    packed = jnp.concatenate([rest[GRAM - LEFT], rest[GRAM + 1 - LEFT]], axis=0)
    turned = pltpu.roll(packed, 64, 1)
    row = lax.broadcasted_iota(jnp.int32, (RANK, 128), 0)
    lane = lax.broadcasted_iota(jnp.int32, (RANK, 128), 1)
    gram = jnp.concatenate([packed, turned], axis=0)
    unit = jnp.where(row == lax.rem(lane, RANK), 1.0, 0.0)
    work = jnp.where(lane < 64, gram, unit)
    first = lax.rem(lane, 64) < RANK
    for step in range(RANK - 1):
        column = jnp.where(
            first,
            jnp.broadcast_to(work[:, step : step + 1], (RANK, 128)),
            jnp.broadcast_to(work[:, RANK + step : RANK + step + 1], (RANK, 128)),
        )
        pivot = work[step : step + 1] / column[step : step + 1]
        work = work - jnp.where(row > step, column, 0.0) * pivot
    diagonal = [
        jnp.sum(jnp.where(lane == row + l * RANK, work, 0.0), axis=1, keepdims=True)
        for l in range(LAYERS)
    ]
    root = jnp.where(
        first,
        jnp.broadcast_to(diagonal[0], (RANK, 128)),
        jnp.broadcast_to(diagonal[1], (RANK, 128)),
    )
    inverse = pltpu.roll(work / jnp.sqrt(root), 64, 1)
    left = jnp.concatenate(
        [jnp.where(lane < RANK, inverse, 0.0), jnp.where((lane >= RANK) & (lane < 64), inverse, 0.0)],
        axis=0,
    )
    scale = rest[SCALE - LEFT]
    out[0] = jnp.concatenate([left[:RANK] * scale[0:1], left[RANK:] * scale[4:5]], axis=0)
    out[1] = left * math.sqrt(COLS)


def invert(rest):
    return pl.pallas_call(
        invert_kernel,
        in_specs=[whole()],
        out_specs=whole(),
        out_shape=jax.ShapeDtypeStruct((2, 64, 128), F32),
        compiler_params=params(),
        cost_estimate=pl.CostEstimate(flops=2_000_000, bytes_accessed=20_000_000, transcendentals=0),
        name="invert_triangle",
    )(rest)


def apply_kernel(which, tiles, inverse, out):
    rows = rows_of([tiles[t, which] for t in range(TILES)])
    done = jnp.dot(
        inverse[which][:, :64], rows, precision=lax.Precision.HIGHEST, preferred_element_type=F32
    )
    for copy in range(out.shape[0]):
        out[copy] = done


def apply(which, copies, tiles, inverse):
    return pl.pallas_call(
        functools.partial(apply_kernel, which),
        in_specs=[whole(), whole()],
        out_specs=whole(),
        out_shape=jax.ShapeDtypeStruct((copies, LAYERS * RANK, ROWS), F32),
        compiler_params=params(),
        name="apply_left" if which else "apply_right",
    )(tiles, inverse)


def assemble_kernel(mine, other, out, sems):
    core = lax.axis_index("core")
    copies = []
    for i, (piece, half) in enumerate(((mine, core), (other, 1 - core))):
        for y in range(YS):
            columns = pl.ds(pl.multiple_of(half * HALF + y * ROWS, 128), ROWS)
            copies.append(pltpu.make_async_copy(piece.at[y], out.at[:, columns], sems.at[i, y]))
    for copy in copies:
        copy.start()
    for copy in copies:
        copy.wait()


def assemble(mine, other):
    return pl.pallas_call(
        assemble_kernel,
        in_specs=[whole(), whole()],
        out_specs=whole(pltpu.HBM),
        out_shape=jax.ShapeDtypeStruct((LAYERS * RANK, COLS), F32),
        scratch_shapes=[pltpu.SemaphoreType.DMA((2, YS))],
        compiler_params=params(),
        name="assemble_right",
    )(mine, other)


def sum_kernel(pieces, *refs):
    out = refs[-1]
    total = functools.reduce(jnp.add, [pieces[r] for r in range(REP)])
    if len(refs) == 1:
        for r in range(REP):
            out[r] = total
    else:
        rest = refs[0]
        for r in range(REP):
            out[r, 0] = total
            out[r, 1] = rest[0]


def sum_and_copy(pieces, rest=None):
    shape = (REP, 8, 128) if rest is None else (REP, 2, 8, 128)
    operands = (pieces,) if rest is None else (pieces, rest)
    return pl.pallas_call(
        sum_kernel,
        in_specs=[whole()] * len(operands),
        out_specs=whole(),
        out_shape=jax.ShapeDtypeStruct(shape, F32),
        compiler_params=params(),
        name="add_replicas",
    )(*operands)


def exchange(value, axis):
    return lax.all_to_all(value, axis, split_axis=0, concat_axis=0, tiled=True)


def swap(value):
    return lax.ppermute(value, "core", [(0, 1), (1, 0)])


def shards(gradient, error_buffer, previous_q, run_starts, run_owners):
    rep = ("x", "z")
    q = jnp.swapaxes(previous_q, 1, 2)
    merged, partial, dest = merge(gradient, error_buffer, q, run_starts, run_owners)
    tiles = exchange(sum_and_copy(exchange(partial, rep)), rep)
    sent = swap(product(False, dest, tiles, merged))
    pieces = exchange(pair(product(True, dest, tiles, merged), sent), "y")
    terms, rest = line(pieces)
    inverse = invert(rest)
    tiles = exchange(sum_and_copy(exchange(terms, rep), rest), rep)
    right = exchange(apply(0, YS, tiles, inverse), "y")
    left = apply(1, 1, tiles, inverse)
    right = assemble(right, swap(right))
    shape = (LAYERS, RANK, -1)
    return tuple(jnp.swapaxes(value.reshape(shape), 1, 2) for value in (left, right))


def solution(mesh):
    grid = jax.sharding.Mesh(mesh.devices.reshape(4, 8, YS, 2), ("x", "z", "y", "core"))
    rep, shard = ("x", "z"), ("y", "core")
    return jax.shard_map(
        shards,
        mesh=grid,
        in_specs=(P(rep, None, shard, None), P(rep, None, shard, None), P(), P(), P()),
        out_specs=(P(None, shard, None), P()),
        check_vma=False,
    )
```

```python
import functools
import math

import jax
import jax.numpy as jnp
from jax import lax
from jax.experimental import pallas as pl
from jax.experimental.pallas import tpu as pltpu
from jax.sharding import PartitionSpec as P

LAYERS = 2
RANK = 32
RANKS = LAYERS * RANK
ROWS = 384
COLS = 3072
HALF = COLS // 2
XS, ZS, YS = 4, 8, 4
PART = RANKS // XS
LEFT, REST = RANKS, RANKS + PART
SENT = REST + 8
CHUNK = 512
CHUNKS = COLS // CHUNK
RUNS = 4
VMEM_LIMIT = 24 * 1024 * 1024
F32 = jnp.float32
BF16 = jnp.bfloat16


def whole(memory_space=pltpu.VMEM):
    return pl.BlockSpec(memory_space=memory_space)


def params(**more):
    return pltpu.CompilerParams(vmem_limit_bytes=VMEM_LIMIT, **more)


def split3(value):
    high = value.astype(BF16)
    rest = value - high.astype(F32)
    middle = rest.astype(BF16)
    low = (rest - middle.astype(F32)).astype(BF16)
    return high, middle, low


def dot_rows(left, right):
    return lax.dot_general(left, right, (((1,), (1,)), ((), ())), preferred_element_type=F32)


def merge_kernel(
    gradient, error, q, starts, owners, merged, partial, dest, g, e, q_in, table, sems, table_sems
):
    tables = [
        pltpu.make_async_copy(source, table.at[i], table_sems.at[i])
        for i, source in enumerate((starts, owners))
    ]
    for copy in tables:
        copy.start()
    copies = []
    for layer in range(LAYERS):
        copies.append([pltpu.make_async_copy(q.at[layer], q_in.at[layer], sems.at[layer, CHUNKS, 0])])
        for chunk in range(CHUNKS):
            columns = pl.ds(chunk * CHUNK, CHUNK)
            copies.append(
                [
                    pltpu.make_async_copy(
                        source.at[0, layer, :, columns],
                        into.at[layer, chunk],
                        sems.at[layer, chunk, i],
                    )
                    for i, (source, into) in enumerate(((gradient, g), (error, e)))
                ]
            )
    for group in copies:
        for copy in group:
            copy.start()
    for copy in tables:
        copy.wait()
    dest[...] = destinations(table)
    arrived = iter(copies)
    for layer in range(LAYERS):
        for copy in next(arrived):
            copy.wait()
        terms = jnp.zeros((RANK, ROWS), F32)
        for chunk in range(CHUNKS):
            for copy in next(arrived):
                copy.wait()
            total = (g[layer, chunk].astype(F32) + e[layer, chunk].astype(F32)).astype(BF16)
            columns = slice(chunk * CHUNK, chunk * CHUNK + CHUNK)
            merged[layer, :, columns] = total
            terms = terms + dot_rows(q_in[layer, :, columns].astype(BF16), total)
        partial[layer * RANK : layer * RANK + RANK] = terms


def destinations(table):
    shard = lax.axis_index("y") * 2 + lax.axis_index("core")
    first = shard * RUNS
    mine = [table[1, first + t] for t in range(RUNS)]

    def count(run, before):
        length = table[0, run + 1] - table[0, run]
        return tuple(b + jnp.where(table[1, run] == o, length, 0) for b, o in zip(before, mine))

    before = lax.fori_loop(0, first, count, (jnp.int32(0),) * RUNS)
    position = shard * ROWS + lax.broadcasted_iota(jnp.int32, (8, ROWS), 1)
    place = position
    for t in range(RUNS):
        start = table[0, first + t]
        moved = position + (mine[t] * ROWS + before[t] - start)
        place = jnp.where(position >= start, moved, place)
    return place


def merge(gradient, error, q, run_starts, run_owners):
    operands = [
        pltpu.with_memory_space_constraint(value, pltpu.HBM)
        for value in (gradient, error, q, run_starts, run_owners)
    ]
    return pl.pallas_call(
        merge_kernel,
        in_specs=[whole(pltpu.HBM)] * 5,
        out_specs=[whole()] * 3,
        out_shape=[
            pltpu.VMEM((LAYERS, ROWS, COLS), BF16),
            jax.ShapeDtypeStruct((RANKS, ROWS), F32),
            jax.ShapeDtypeStruct((8, ROWS), jnp.int32),
        ],
        scratch_shapes=[
            pltpu.VMEM((LAYERS, CHUNKS, ROWS, CHUNK), BF16),
            pltpu.VMEM((LAYERS, CHUNKS, ROWS, CHUNK), BF16),
            pltpu.VMEM((LAYERS, RANK, COLS), F32),
            pltpu.SMEM((2, 2 * YS * RUNS), jnp.int32),
            pltpu.SemaphoreType.DMA((LAYERS, CHUNKS + 1, 2)),
            pltpu.SemaphoreType.DMA((2,)),
        ],
        compiler_params=params(),
        name="merge_project",
    )(*operands)


def product_kernel(own, dest, factor_in, merged, out):
    at = lax.axis_index("y")
    half = lax.axis_index("core") if own else 1 - lax.axis_index("core")
    factor = factor_in[...]
    biggest = [
        jnp.max(jnp.abs(factor[l * RANK : l * RANK + RANK]), keepdims=True) for l in range(LAYERS)
    ]
    scales = [jnp.where(b > 0, b * 64.0, 1.0) for b in biggest]
    columns = pl.ds(pl.multiple_of(half * HALF, 128), HALF)
    step = [lax.rem(y - at + YS, YS) for y in range(YS)]
    for layer in range(LAYERS):
        ranks = slice(layer * RANK, layer * RANK + RANK)
        parts = jnp.concatenate(split3(factor[ranks] * (1.0 / scales[layer])), axis=0)
        product = jnp.dot(parts, merged[layer, :, columns], preferred_element_type=F32)
        product = product[:RANK] + product[RANK : 2 * RANK] + product[2 * RANK :]
        for y in range(YS):
            out[step[y], ranks] = product[:, y * ROWS : y * ROWS + ROWS]
    first = pl.multiple_of(lax.axis_index("x") * PART, PART)
    rows = jnp.concatenate(split3(factor_in[pl.ds(first, PART)]), axis=0)
    wanted = jnp.broadcast_to(dest[0:1], (ROWS, ROWS)) - lax.broadcasted_iota(
        jnp.int32, (ROWS, ROWS), 0
    )
    for y in range(YS):
        chosen = jnp.where(wanted == (y * 2 + half) * ROWS, 1.0, 0.0).astype(BF16)
        found = dot_rows(rows, chosen)
        out[step[y], LEFT:REST] = found[:PART] + found[PART : 2 * PART] + found[2 * PART :]
    high, middle, low = split3(factor)
    left = jnp.concatenate([high, middle, low], axis=0)
    right = jnp.concatenate([high, high, middle, middle, low, low], axis=0)
    gram = dot_rows(left, right)
    gram = gram[:64] + gram[64:128] + gram[128:]
    gram = gram[:, :128] + gram[:, 128:256] + gram[:, 256:]
    lane = lax.broadcasted_iota(jnp.int32, (RANK, 128), 1)
    gram = jnp.where(lax.rem(lane, 64) < 32, gram[:RANK], gram[RANK:])
    gram = jnp.where(lane[:16] < 64, gram[:16], gram[16:])
    scale = jnp.concatenate([jnp.broadcast_to(s, (4, 128)) for s in scales], axis=0)
    rest = jnp.concatenate([gram[:8], gram[8:], scale], axis=1)
    for k in range(YS):
        out[k, REST:] = rest


def product(own, dest, factor, merged):
    return pl.pallas_call(
        functools.partial(product_kernel, own),
        in_specs=[whole()] * 3,
        out_specs=whole(),
        out_shape=jax.ShapeDtypeStruct((YS, SENT, ROWS), F32),
        compiler_params=params(),
        name="product_own_half" if own else "product_other_half",
    )(dest, factor, pltpu.with_memory_space_constraint(merged, pltpu.VMEM))


def add_scaled(pieces):
    scales = [p[REST:, 256:] for p in pieces]
    largest = functools.reduce(jnp.maximum, scales)
    ratios = [scale / largest for scale in scales]
    products = []
    for layer in range(LAYERS):
        ranks = slice(layer * RANK, layer * RANK + RANK)
        terms = []
        for piece, ratio in zip(pieces, ratios):
            row = jnp.broadcast_to(ratio[4 * layer : 4 * layer + 1], (RANK, 128))
            terms.append(piece[ranks] * jnp.concatenate([row] * (ROWS // 128), axis=1))
        products.append(functools.reduce(jnp.add, terms))
    left = functools.reduce(jnp.add, [p[LEFT:REST] for p in pieces])
    gram = functools.reduce(jnp.add, [p[REST:, :256] for p in pieces])
    return products, left, jnp.concatenate([gram, largest], axis=1)


def store_scaled(pieces, out, rest):
    products, left, last = add_scaled(pieces)
    for layer in range(LAYERS):
        out[layer * RANK : layer * RANK + RANK] = products[layer]
    out[LEFT:REST] = left
    rest[...] = last


def pair_kernel(mine, other, *outs):
    for k, out in enumerate(outs):
        store_scaled([mine.at[k], other.at[k]], out, out.at[REST:])


def pair(mine, other):
    return pl.pallas_call(
        pair_kernel,
        in_specs=[whole(), whole()],
        out_specs=[whole()] * YS,
        out_shape=[jax.ShapeDtypeStruct((SENT, ROWS), F32)] * YS,
        compiler_params=params(),
        name="add_cores",
    )(mine, other)


def line_kernel(a, b, c, d, out, rest):
    store_scaled([a, b, c, d], out, rest)


def line(pieces):
    return pl.pallas_call(
        line_kernel,
        in_specs=[whole()] * YS,
        out_specs=[whole(), whole()],
        out_shape=[
            jax.ShapeDtypeStruct((REST, ROWS), F32),
            jax.ShapeDtypeStruct((SENT - REST, ROWS), F32),
        ],
        compiler_params=params(),
        name="add_line",
    )(*pieces)


def cross_kernel(own, *refs):
    *others, out, left = refs
    pieces = [own, *others]
    out[...] = (own[:LEFT] + others[1][:LEFT]) + (others[0][:LEFT] + others[2][:LEFT])
    for k, piece in enumerate(pieces):
        part = lax.rem(lax.axis_index("x") - k + XS, XS)
        left[pl.ds(pl.multiple_of(part * PART, PART), PART)] = piece[LEFT:REST]


def cross(pieces):
    return pl.pallas_call(
        cross_kernel,
        in_specs=[whole()] * XS,
        out_specs=[whole(), whole()],
        out_shape=[jax.ShapeDtypeStruct((RANKS, ROWS), F32)] * 2,
        compiler_params=params(),
        name="add_cross",
    )(*pieces)


def add_kernel(*refs):
    *pieces, out = refs
    while len(pieces) > 1:
        pieces = [a[...] + b[...] for a, b in zip(pieces[::2], pieces[1::2])]
    out[...] = pieces[0]


def add(*pieces):
    return pl.pallas_call(
        add_kernel,
        in_specs=[whole()] * len(pieces),
        out_specs=whole(),
        out_shape=jax.ShapeDtypeStruct((RANKS, ROWS), F32),
        compiler_params=params(),
        name="add_pieces",
    )(*pieces)


def invert_kernel(rest, out):
    packed = jnp.concatenate([rest[:, :128], rest[:, 128:256]], axis=0)
    turned = pltpu.roll(packed, 64, 1)
    row = lax.broadcasted_iota(jnp.int32, (RANK, 128), 0)
    lane = lax.broadcasted_iota(jnp.int32, (RANK, 128), 1)
    gram = jnp.concatenate([packed, turned], axis=0)
    unit = jnp.where(row == lax.rem(lane, RANK), 1.0, 0.0)
    work = jnp.where(lane < 64, gram, unit)
    first = lax.rem(lane, 64) < RANK
    for step in range(RANK - 1):
        column = jnp.where(
            first,
            jnp.broadcast_to(work[:, step : step + 1], (RANK, 128)),
            jnp.broadcast_to(work[:, RANK + step : RANK + step + 1], (RANK, 128)),
        )
        pivot = work[step : step + 1] / column[step : step + 1]
        work = work - jnp.where(row > step, column, 0.0) * pivot
    diagonal = [
        jnp.sum(jnp.where(lane == row + l * RANK, work, 0.0), axis=1, keepdims=True)
        for l in range(LAYERS)
    ]
    root = jnp.where(
        first,
        jnp.broadcast_to(diagonal[0], (RANK, 128)),
        jnp.broadcast_to(diagonal[1], (RANK, 128)),
    )
    inverse = pltpu.roll(work / jnp.sqrt(root), 64, 1)
    left = jnp.concatenate(
        [jnp.where(lane < RANK, inverse, 0.0), jnp.where((lane >= RANK) & (lane < 64), inverse, 0.0)],
        axis=0,
    )
    scale = rest[:, 256:]
    out[0] = jnp.concatenate([left[:RANK] * scale[0:1], left[RANK:] * scale[4:5]], axis=0)
    out[1] = left * math.sqrt(COLS)


def invert(rest):
    return pl.pallas_call(
        invert_kernel,
        in_specs=[whole()],
        out_specs=whole(),
        out_shape=jax.ShapeDtypeStruct((2, 64, 128), F32),
        compiler_params=params(),
        cost_estimate=pl.CostEstimate(flops=2_000_000, bytes_accessed=20_000_000, transcendentals=0),
        name="invert_triangle",
    )(rest)


def apply_kernel(which, rows, inverse, out):
    out[...] = jnp.dot(
        inverse[which][:, :RANKS],
        rows[...],
        precision=lax.Precision.HIGHEST,
        preferred_element_type=F32,
    )


def apply(which, rows, inverse):
    return pl.pallas_call(
        functools.partial(apply_kernel, which),
        in_specs=[whole(), whole()],
        out_specs=whole(),
        out_shape=jax.ShapeDtypeStruct((RANKS, ROWS), F32),
        compiler_params=params(),
        name="apply_left" if which else "apply_right",
    )(rows, inverse)


def assemble_kernel(*refs):
    *pieces, out, sems = refs
    core, at = lax.axis_index("core"), lax.axis_index("y")
    copies = []
    for i, piece in enumerate(pieces):
        half = core if i < YS else 1 - core
        block = lax.rem(at - i % YS + YS, YS)
        columns = pl.ds(pl.multiple_of(half * HALF + block * ROWS, 128), ROWS)
        copies.append(pltpu.make_async_copy(piece, out.at[:, columns], sems.at[i]))
    for copy in copies:
        copy.start()
    for copy in copies:
        copy.wait()


def assemble(pieces):
    return pl.pallas_call(
        assemble_kernel,
        in_specs=[whole()] * (2 * YS),
        out_specs=whole(pltpu.HBM),
        out_shape=jax.ShapeDtypeStruct((RANKS, COLS), F32),
        scratch_shapes=[pltpu.SemaphoreType.DMA((2 * YS,))],
        compiler_params=params(),
        name="assemble_right",
    )(*pieces)


def swap(value):
    return lax.ppermute(value, "core", [(0, 1), (1, 0)])


def rotate(value, axis, step):
    size = lax.axis_size(axis)
    return lax.ppermute(value, axis, [(i, (i + step) % size) for i in range(size)])


def along_z(value, even, odd):
    sources = [(z + (odd if z % 2 else even)) % ZS for z in range(ZS)]
    return lax.ppermute(value, "z", [(source, z) for z, source in enumerate(sources)])


def sum_z(value):
    value = add(value, along_z(value, 1, -1))
    return add(value, along_z(value, -3, 3), along_z(value, -1, 1), along_z(value, 2, -2))


def shards(gradient, error_buffer, previous_q, run_starts, run_owners):
    q = jnp.swapaxes(previous_q, 1, 2)
    merged, partial, dest = merge(gradient, error_buffer, q, run_starts, run_owners)
    far, near, back = [rotate(partial, "x", step) for step in (2, 1, 3)]
    factor = sum_z(add(partial, far, near, back))
    sent = swap(product(False, dest, factor, merged))
    pieces = pair(product(True, dest, factor, merged), sent)
    pieces = [pieces[0]] + [rotate(pieces[k], "y", k) for k in range(1, YS)]
    terms, rest = line(pieces)
    inverse = invert(rest)
    terms, rows = cross([terms] + [rotate(terms, "x", k) for k in range(1, XS)])
    right = apply(0, sum_z(terms), inverse)
    left = apply(1, rows, inverse)
    right = [right] + [rotate(right, "y", k) for k in range(1, YS)]
    right = assemble(right + [swap(value) for value in right])
    shape = (LAYERS, RANK, -1)
    return tuple(jnp.swapaxes(value.reshape(shape), 1, 2) for value in (left, right))


def solution(mesh):
    grid = jax.sharding.Mesh(mesh.devices.reshape(XS, ZS, YS, 2), ("x", "z", "y", "core"))
    rep, shard = ("x", "z"), ("y", "core")
    return jax.shard_map(
        shards,
        mesh=grid,
        in_specs=(P(rep, None, shard, None), P(rep, None, shard, None), P(), P(), P()),
        out_specs=(P(None, shard, None), P()),
        check_vma=False,
    )
```

```python
import functools
import math

import jax
import jax.numpy as jnp
from jax import lax
from jax.experimental import pallas as pl
from jax.experimental.pallas import tpu as pltpu
from jax.sharding import PartitionSpec as P

LAYERS = 2
RANK = 32
RANKS = LAYERS * RANK
ROWS = 384
COLS = 3072
HALF = COLS // 2
XS, ZS, YS = 4, 8, 4
PART = RANKS // XS
LEFT, REST = RANKS, RANKS + PART
SENT = REST + 8
CHUNK = 512
CHUNKS = COLS // CHUNK
RUNS = 4
AHEAD = (0, 1, 3, 2)
VMEM_LIMIT = 24 * 1024 * 1024
F32 = jnp.float32
BF16 = jnp.bfloat16


def whole(memory_space=pltpu.VMEM):
    return pl.BlockSpec(memory_space=memory_space)


def params(**more):
    return pltpu.CompilerParams(vmem_limit_bytes=VMEM_LIMIT, **more)


def split3(value):
    high = value.astype(BF16)
    rest = value - high.astype(F32)
    middle = rest.astype(BF16)
    low = (rest - middle.astype(F32)).astype(BF16)
    return high, middle, low


def dot_rows(left, right):
    return lax.dot_general(left, right, (((1,), (1,)), ((), ())), preferred_element_type=F32)


def merge_kernel(
    gradient, error, q, starts, owners, merged, partial, dest, g, e, q_in, table, sems, table_sems
):
    tables = [
        pltpu.make_async_copy(source, table.at[i], table_sems.at[i])
        for i, source in enumerate((starts, owners))
    ]
    for copy in tables:
        copy.start()
    copies = []
    for layer in range(LAYERS):
        copies.append([pltpu.make_async_copy(q.at[layer], q_in.at[layer], sems.at[layer, CHUNKS, 0])])
        for chunk in range(CHUNKS):
            columns = pl.ds(chunk * CHUNK, CHUNK)
            copies.append(
                [
                    pltpu.make_async_copy(
                        source.at[0, layer, :, columns],
                        into.at[layer, chunk],
                        sems.at[layer, chunk, i],
                    )
                    for i, (source, into) in enumerate(((gradient, g), (error, e)))
                ]
            )
    for group in copies:
        for copy in group:
            copy.start()
    for copy in tables:
        copy.wait()
    dest[...] = destinations(table)
    arrived = iter(copies)
    for layer in range(LAYERS):
        for copy in next(arrived):
            copy.wait()
        terms = jnp.zeros((RANK, ROWS), F32)
        for chunk in range(CHUNKS):
            for copy in next(arrived):
                copy.wait()
            total = (g[layer, chunk].astype(F32) + e[layer, chunk].astype(F32)).astype(BF16)
            columns = slice(chunk * CHUNK, chunk * CHUNK + CHUNK)
            merged[layer, :, columns] = total
            terms = terms + dot_rows(q_in[layer, :, columns].astype(BF16), total)
        partial[layer * RANK : layer * RANK + RANK] = terms


def destinations(table):
    shard = lax.axis_index("y") * 2 + lax.axis_index("core")
    first = shard * RUNS
    mine = [table[1, first + t] for t in range(RUNS)]

    def count(run, before):
        length = table[0, run + 1] - table[0, run]
        return tuple(b + jnp.where(table[1, run] == o, length, 0) for b, o in zip(before, mine))

    before = lax.fori_loop(0, first, count, (jnp.int32(0),) * RUNS)
    position = shard * ROWS + lax.broadcasted_iota(jnp.int32, (8, ROWS), 1)
    place = position
    for t in range(RUNS):
        start = table[0, first + t]
        moved = position + (mine[t] * ROWS + before[t] - start)
        place = jnp.where(position >= start, moved, place)
    return place


def merge(gradient, error, q, run_starts, run_owners):
    operands = [
        pltpu.with_memory_space_constraint(value, pltpu.HBM)
        for value in (gradient, error, q, run_starts, run_owners)
    ]
    return pl.pallas_call(
        merge_kernel,
        in_specs=[whole(pltpu.HBM)] * 5,
        out_specs=[whole()] * 3,
        out_shape=[
            pltpu.VMEM((LAYERS, ROWS, COLS), BF16),
            jax.ShapeDtypeStruct((RANKS, ROWS), F32),
            jax.ShapeDtypeStruct((8, ROWS), jnp.int32),
        ],
        scratch_shapes=[
            pltpu.VMEM((LAYERS, CHUNKS, ROWS, CHUNK), BF16),
            pltpu.VMEM((LAYERS, CHUNKS, ROWS, CHUNK), BF16),
            pltpu.VMEM((LAYERS, RANK, COLS), F32),
            pltpu.SMEM((2, 2 * YS * RUNS), jnp.int32),
            pltpu.SemaphoreType.DMA((LAYERS, CHUNKS + 1, 2)),
            pltpu.SemaphoreType.DMA((2,)),
        ],
        compiler_params=params(),
        name="merge_project",
    )(*operands)


def product_kernel(own, dest, factor_in, merged, out):
    at = lax.axis_index("y")
    half = lax.axis_index("core") if own else 1 - lax.axis_index("core")
    factor = factor_in[...]
    biggest = [
        jnp.max(jnp.abs(factor[l * RANK : l * RANK + RANK]), keepdims=True) for l in range(LAYERS)
    ]
    scales = [jnp.where(b > 0, b * 64.0, 1.0) for b in biggest]
    columns = pl.ds(pl.multiple_of(half * HALF, 128), HALF)
    step = [lax.rem(y - at + YS, YS) for y in range(YS)]
    for layer in range(LAYERS):
        ranks = slice(layer * RANK, layer * RANK + RANK)
        parts = jnp.concatenate(split3(factor[ranks] * (1.0 / scales[layer])), axis=0)
        product = jnp.dot(parts, merged[layer, :, columns], preferred_element_type=F32)
        product = product[:RANK] + product[RANK : 2 * RANK] + product[2 * RANK :]
        for y in range(YS):
            out[step[y], ranks] = product[:, y * ROWS : y * ROWS + ROWS]
    first = pl.multiple_of(lax.axis_index("x") * PART, PART)
    rows = jnp.concatenate(split3(factor_in[pl.ds(first, PART)]), axis=0)
    wanted = jnp.broadcast_to(dest[0:1], (ROWS, ROWS)) - lax.broadcasted_iota(
        jnp.int32, (ROWS, ROWS), 0
    )
    for y in range(YS):
        chosen = jnp.where(wanted == (y * 2 + half) * ROWS, 1.0, 0.0).astype(BF16)
        found = dot_rows(rows, chosen)
        out[step[y], LEFT:REST] = found[:PART] + found[PART : 2 * PART] + found[2 * PART :]
    high, middle, low = split3(factor)
    left = jnp.concatenate([high, middle, low], axis=0)
    right = jnp.concatenate([high, high, middle, middle, low, low], axis=0)
    gram = dot_rows(left, right)
    gram = gram[:64] + gram[64:128] + gram[128:]
    gram = gram[:, :128] + gram[:, 128:256] + gram[:, 256:]
    lane = lax.broadcasted_iota(jnp.int32, (RANK, 128), 1)
    gram = jnp.where(lax.rem(lane, 64) < 32, gram[:RANK], gram[RANK:])
    gram = jnp.where(lane[:16] < 64, gram[:16], gram[16:])
    scale = jnp.concatenate([jnp.broadcast_to(s, (4, 128)) for s in scales], axis=0)
    rest = jnp.concatenate([gram[:8], gram[8:], scale], axis=1)
    for k in range(YS):
        out[k, REST:] = rest


def product(own, dest, factor, merged):
    return pl.pallas_call(
        functools.partial(product_kernel, own),
        in_specs=[whole()] * 3,
        out_specs=whole(),
        out_shape=jax.ShapeDtypeStruct((YS, SENT, ROWS), F32),
        compiler_params=params(),
        name="product_own_half" if own else "product_other_half",
    )(dest, factor, pltpu.with_memory_space_constraint(merged, pltpu.VMEM))


def add_scaled(pieces):
    scales = [p[REST:, 256:] for p in pieces]
    largest = functools.reduce(jnp.maximum, scales)
    ratios = [scale / largest for scale in scales]
    products = []
    for layer in range(LAYERS):
        ranks = slice(layer * RANK, layer * RANK + RANK)
        terms = []
        for piece, ratio in zip(pieces, ratios):
            row = jnp.broadcast_to(ratio[4 * layer : 4 * layer + 1], (RANK, 128))
            terms.append(piece[ranks] * jnp.concatenate([row] * (ROWS // 128), axis=1))
        products.append(functools.reduce(jnp.add, terms))
    left = functools.reduce(jnp.add, [p[LEFT:REST] for p in pieces])
    gram = functools.reduce(jnp.add, [p[REST:, :256] for p in pieces])
    return products, left, jnp.concatenate([gram, largest], axis=1)


def store_scaled(pieces, out, rest):
    products, left, last = add_scaled(pieces)
    for layer in range(LAYERS):
        out[layer * RANK : layer * RANK + RANK] = products[layer]
    out[LEFT:REST] = left
    rest[...] = last


def pair_kernel(mine, other, *outs):
    for k, out in enumerate(outs):
        store_scaled([mine.at[k], other.at[k]], out, out.at[REST:])


def pair(mine, other):
    return pl.pallas_call(
        pair_kernel,
        in_specs=[whole(), whole()],
        out_specs=[whole()] * YS,
        out_shape=[jax.ShapeDtypeStruct((SENT, ROWS), F32)] * YS,
        compiler_params=params(),
        name="add_cores",
    )(mine, other)


def line_kernel(a, b, c, d, out, rest):
    store_scaled([a, b, c, d], out, rest)


def line(pieces):
    return pl.pallas_call(
        line_kernel,
        in_specs=[whole()] * YS,
        out_specs=[whole(), whole()],
        out_shape=[
            jax.ShapeDtypeStruct((REST, ROWS), F32),
            jax.ShapeDtypeStruct((SENT - REST, ROWS), F32),
        ],
        compiler_params=params(),
        name="add_line",
    )(*pieces)


def cross_kernel(own, *refs):
    *others, out, left = refs
    near, back, far = others
    out[...] = (own[:LEFT] + far[:LEFT]) + (near[:LEFT] + back[:LEFT])
    for k, piece in zip(AHEAD, (own, *others)):
        part = lax.rem(lax.axis_index("x") - k + XS, XS)
        left[pl.ds(pl.multiple_of(part * PART, PART), PART)] = piece[LEFT:REST]


def cross(pieces):
    return pl.pallas_call(
        cross_kernel,
        in_specs=[whole()] * XS,
        out_specs=[whole(), whole()],
        out_shape=[jax.ShapeDtypeStruct((RANKS, ROWS), F32)] * 2,
        compiler_params=params(),
        name="add_cross",
    )(*pieces)


def add_kernel(*refs):
    *pieces, out = refs
    if len(pieces) == 2:
        out[...] = pieces[0][...] + pieces[1][...]
    else:
        first, second, third, last = pieces
        out[...] = (first[...] + last[...]) + (second[...] + third[...])


def add(*pieces):
    return pl.pallas_call(
        add_kernel,
        in_specs=[whole()] * len(pieces),
        out_specs=whole(),
        out_shape=jax.ShapeDtypeStruct((RANKS, ROWS), F32),
        compiler_params=params(),
        name="add_pieces",
    )(*pieces)


def invert_kernel(rest, rows, out, left_out):
    packed = jnp.concatenate([rest[:, :128], rest[:, 128:256]], axis=0)
    turned = pltpu.roll(packed, 64, 1)
    row = lax.broadcasted_iota(jnp.int32, (RANK, 128), 0)
    lane = lax.broadcasted_iota(jnp.int32, (RANK, 128), 1)
    gram = jnp.concatenate([packed, turned], axis=0)
    unit = jnp.where(row == lax.rem(lane, RANK), 1.0, 0.0)
    work = jnp.where(lane < 64, gram, unit)
    first = lax.rem(lane, 64) < RANK
    for step in range(RANK - 1):
        column = jnp.where(
            first,
            jnp.broadcast_to(work[:, step : step + 1], (RANK, 128)),
            jnp.broadcast_to(work[:, RANK + step : RANK + step + 1], (RANK, 128)),
        )
        pivot = work[step : step + 1] / column[step : step + 1]
        work = work - jnp.where(row > step, column, 0.0) * pivot
    diagonal = [
        jnp.sum(jnp.where(lane == row + l * RANK, work, 0.0), axis=1, keepdims=True)
        for l in range(LAYERS)
    ]
    root = jnp.where(
        first,
        jnp.broadcast_to(diagonal[0], (RANK, 128)),
        jnp.broadcast_to(diagonal[1], (RANK, 128)),
    )
    inverse = pltpu.roll(work / jnp.sqrt(root), 64, 1)
    left = jnp.concatenate(
        [jnp.where(lane < RANK, inverse, 0.0), jnp.where((lane >= RANK) & (lane < 64), inverse, 0.0)],
        axis=0,
    )
    scale = rest[:, 256:]
    out[...] = jnp.concatenate([left[:RANK] * scale[0:1], left[RANK:] * scale[4:5]], axis=0)
    left_out[...] = multiply(left * math.sqrt(COLS), rows[...])


def multiply(triangle, rows):
    return jnp.dot(
        triangle[:, :RANKS], rows, precision=lax.Precision.HIGHEST, preferred_element_type=F32
    )


def invert(rest, rows):
    return pl.pallas_call(
        invert_kernel,
        in_specs=[whole()] * 2,
        out_specs=[whole()] * 2,
        out_shape=[
            jax.ShapeDtypeStruct((RANKS, 128), F32),
            jax.ShapeDtypeStruct((RANKS, ROWS), F32),
        ],
        compiler_params=params(),
        cost_estimate=pl.CostEstimate(flops=2_000_000, bytes_accessed=20_000_000, transcendentals=0),
        name="invert_triangle",
    )(rest, rows)


def apply_kernel(rows, inverse, out):
    out[...] = multiply(inverse, rows[...])


def apply(rows, inverse):
    return pl.pallas_call(
        apply_kernel,
        in_specs=[whole(), whole()],
        out_specs=whole(),
        out_shape=jax.ShapeDtypeStruct((RANKS, ROWS), F32),
        compiler_params=params(),
        name="apply_right",
    )(rows, inverse)


def assemble_kernel(swapped, *refs):
    *pieces, out, sems = refs
    core, at = lax.axis_index("core"), lax.axis_index("y")
    half = 1 - core if swapped else core
    copies = []
    for k, piece in enumerate(pieces[-YS:]):
        block = lax.rem(at - k + YS, YS)
        columns = pl.ds(pl.multiple_of(half * HALF + block * ROWS, 128), ROWS)
        copies.append(pltpu.make_async_copy(piece, out.at[:, columns], sems.at[k]))
    for copy in copies:
        copy.start()
    for copy in copies:
        copy.wait()


def assemble(pieces, out=None):
    swapped = out is not None
    return pl.pallas_call(
        functools.partial(assemble_kernel, swapped),
        in_specs=[whole(pltpu.HBM)] * swapped + [whole()] * YS,
        out_specs=whole(pltpu.HBM),
        out_shape=jax.ShapeDtypeStruct((RANKS, COLS), F32),
        scratch_shapes=[pltpu.SemaphoreType.DMA((YS,))],
        compiler_params=params(),
        input_output_aliases={0: 0} if swapped else {},
        name="assemble_other_half" if swapped else "assemble_own_half",
    )(*([out] * swapped), *pieces)


def swap(value):
    return lax.ppermute(value, "core", [(0, 1), (1, 0)])


def rotate(value, axis, step):
    size = lax.axis_size(axis)
    return lax.ppermute(value, axis, [(i, (i + step) % size) for i in range(size)])


def along_z(value, even, odd):
    sources = [(z + (odd if z % 2 else even)) % ZS for z in range(ZS)]
    return lax.ppermute(value, "z", [(source, z) for z, source in enumerate(sources)])


def sum_z(value):
    value = add(value, along_z(value, 1, -1))
    two, near, three = [along_z(value, at, -at) for at in (2, -1, -3)]
    return add(value, two, near, three)


def turns(values, axis, ahead=AHEAD):
    return [values[0]] + [rotate(value, axis, k) for value, k in zip(values[1:], ahead[1:])]


def shards(gradient, error_buffer, previous_q, run_starts, run_owners):
    q = jnp.swapaxes(previous_q, 1, 2)
    merged, partial, dest = merge(gradient, error_buffer, q, run_starts, run_owners)
    factor = sum_z(add(*turns([partial] * XS, "x")))
    sent = swap(product(False, dest, factor, merged))
    pieces = pair(product(True, dest, factor, merged), sent)
    terms, rest = line(turns([pieces[k] for k in (0, 2, 1, 3)], "y", (0, 2, 1, 3)))
    terms, rows = cross(turns([terms] * XS, "x"))
    inverse, left = invert(rest, rows)
    right = apply(sum_z(terms), inverse)
    right = turns([right] * YS, "y", range(YS))
    right = assemble([swap(value) for value in right], assemble(right))
    shape = (LAYERS, RANK, -1)
    return tuple(jnp.swapaxes(value.reshape(shape), 1, 2) for value in (left, right))


def solution(mesh):
    grid = jax.sharding.Mesh(mesh.devices.reshape(XS, ZS, YS, 2), ("x", "z", "y", "core"))
    rep, shard = ("x", "z"), ("y", "core")
    return jax.shard_map(
        shards,
        mesh=grid,
        in_specs=(P(rep, None, shard, None), P(rep, None, shard, None), P(), P(), P()),
        out_specs=(P(None, shard, None), P()),
        check_vma=False,
    )
```

```python
import functools
import math

import jax
import jax.numpy as jnp
from jax import lax
from jax.experimental import pallas as pl
from jax.experimental.pallas import tpu as pltpu
from jax.sharding import PartitionSpec as P

LAYERS = 2
RANK = 32
RANKS = LAYERS * RANK
ROWS = 384
COLS = 3072
HALF = COLS // 2
XS, ZS, YS = 4, 8, 4
PART = RANKS // XS
LEFT, REST = RANKS, RANKS + PART
SENT = REST + 8
CHUNK = 512
CHUNKS = COLS // CHUNK
RUNS = 4
ORDER_FIRST = (0, 2, 3, 1)
ORDER_LINE = (0, 1, 2, 3)
ORDER_CROSS = (0, 2, 3, 1)
ORDER_LAST = (0, 1, 2, 3)
VMEM_LIMIT = 24 * 1024 * 1024
F32 = jnp.float32
BF16 = jnp.bfloat16


def whole(memory_space=pltpu.VMEM):
    return pl.BlockSpec(memory_space=memory_space)


def params(**more):
    return pltpu.CompilerParams(vmem_limit_bytes=VMEM_LIMIT, **more)


def split3(value):
    high = value.astype(BF16)
    rest = value - high.astype(F32)
    middle = rest.astype(BF16)
    low = (rest - middle.astype(F32)).astype(BF16)
    return high, middle, low


def dot_rows(left, right):
    return lax.dot_general(left, right, (((1,), (1,)), ((), ())), preferred_element_type=F32)


def merge_kernel(
    gradient, error, q, starts, owners, merged, partial, dest, g, e, q_in, table, sems, table_sems
):
    tables = [
        pltpu.make_async_copy(source, table.at[i], table_sems.at[i])
        for i, source in enumerate((starts, owners))
    ]
    for copy in tables:
        copy.start()
    copies = []
    for layer in range(LAYERS):
        copies.append([pltpu.make_async_copy(q.at[layer], q_in.at[layer], sems.at[layer, CHUNKS, 0])])
        for chunk in range(CHUNKS):
            columns = pl.ds(chunk * CHUNK, CHUNK)
            copies.append(
                [
                    pltpu.make_async_copy(
                        source.at[0, layer, :, columns],
                        into.at[layer, chunk],
                        sems.at[layer, chunk, i],
                    )
                    for i, (source, into) in enumerate(((gradient, g), (error, e)))
                ]
            )
    for group in copies:
        for copy in group:
            copy.start()
    for copy in tables:
        copy.wait()
    dest[...] = destinations(table)
    arrived = iter(copies)
    for layer in range(LAYERS):
        for copy in next(arrived):
            copy.wait()
        terms = jnp.zeros((RANK, ROWS), F32)
        for chunk in range(CHUNKS):
            for copy in next(arrived):
                copy.wait()
            total = (g[layer, chunk].astype(F32) + e[layer, chunk].astype(F32)).astype(BF16)
            columns = slice(chunk * CHUNK, chunk * CHUNK + CHUNK)
            merged[layer, :, columns] = total
            terms = terms + dot_rows(q_in[layer, :, columns].astype(BF16), total)
        partial[layer * RANK : layer * RANK + RANK] = terms


def destinations(table):
    shard = lax.axis_index("y") * 2 + lax.axis_index("core")
    first = shard * RUNS
    mine = [table[1, first + t] for t in range(RUNS)]

    def count(run, before):
        length = table[0, run + 1] - table[0, run]
        return tuple(b + jnp.where(table[1, run] == o, length, 0) for b, o in zip(before, mine))

    before = lax.fori_loop(0, first, count, (jnp.int32(0),) * RUNS)
    position = shard * ROWS + lax.broadcasted_iota(jnp.int32, (8, ROWS), 1)
    place = position
    for t in range(RUNS):
        start = table[0, first + t]
        moved = position + (mine[t] * ROWS + before[t] - start)
        place = jnp.where(position >= start, moved, place)
    return place


def merge(gradient, error, q, run_starts, run_owners):
    operands = [
        pltpu.with_memory_space_constraint(value, pltpu.HBM)
        for value in (gradient, error, q, run_starts, run_owners)
    ]
    return pl.pallas_call(
        merge_kernel,
        in_specs=[whole(pltpu.HBM)] * 5,
        out_specs=[whole()] * 3,
        out_shape=[
            pltpu.VMEM((LAYERS, ROWS, COLS), BF16),
            jax.ShapeDtypeStruct((RANKS, ROWS), F32),
            jax.ShapeDtypeStruct((8, ROWS), jnp.int32),
        ],
        scratch_shapes=[
            pltpu.VMEM((LAYERS, CHUNKS, ROWS, CHUNK), BF16),
            pltpu.VMEM((LAYERS, CHUNKS, ROWS, CHUNK), BF16),
            pltpu.VMEM((LAYERS, RANK, COLS), F32),
            pltpu.SMEM((2, 2 * YS * RUNS), jnp.int32),
            pltpu.SemaphoreType.DMA((LAYERS, CHUNKS + 1, 2)),
            pltpu.SemaphoreType.DMA((2,)),
        ],
        compiler_params=params(),
        name="merge_project",
    )(*operands)


def prepare_kernel(factor_in, parts, rest):
    factor = factor_in[...]
    biggest = [
        jnp.max(jnp.abs(factor[l * RANK : l * RANK + RANK]), keepdims=True) for l in range(LAYERS)
    ]
    scales = [jnp.where(b > 0, b * 64.0, 1e-30) for b in biggest]
    for layer in range(LAYERS):
        scaled = factor[layer * RANK : layer * RANK + RANK] * (1.0 / scales[layer])
        for i, part in enumerate(split3(scaled)):
            parts[layer, i * RANK : i * RANK + RANK] = part
    high, middle, low = split3(factor)
    left = jnp.concatenate([high, middle, low], axis=0)
    right = jnp.concatenate([high, high, middle, middle, low, low], axis=0)
    gram = dot_rows(left, right)
    gram = gram[:64] + gram[64:128] + gram[128:]
    gram = gram[:, :128] + gram[:, 128:256] + gram[:, 256:]
    lane = lax.broadcasted_iota(jnp.int32, (RANK, 128), 1)
    gram = jnp.where(lax.rem(lane, 64) < 32, gram[:RANK], gram[RANK:])
    gram = jnp.where(lane[:16] < 64, gram[:16], gram[16:])
    scale = jnp.concatenate([jnp.broadcast_to(s, (4, 128)) for s in scales], axis=0)
    rest[...] = jnp.concatenate([gram[:8], gram[8:], scale], axis=1)


def prepare(factor):
    return pl.pallas_call(
        prepare_kernel,
        in_specs=[whole()],
        out_specs=[whole(), whole()],
        out_shape=[
            jax.ShapeDtypeStruct((LAYERS, 3 * RANK, ROWS), BF16),
            jax.ShapeDtypeStruct((8, ROWS), F32),
        ],
        compiler_params=params(),
        name="split_factor",
    )(factor)


def product_kernel(own, steps, dest, factor_in, parts, rest, merged, out):
    half = lax.axis_index("core") if own else 1 - lax.axis_index("core")
    first = pl.multiple_of(lax.axis_index("x") * PART, PART)
    rows = jnp.concatenate(split3(factor_in[pl.ds(first, PART)]), axis=0)
    wanted = jnp.broadcast_to(dest[0:1], (ROWS, ROWS)) - lax.broadcasted_iota(
        jnp.int32, (ROWS, ROWS), 0
    )
    for i, step in enumerate(steps):
        y = lax.rem(lax.axis_index("y") + step, YS)
        columns = pl.ds(pl.multiple_of(half * HALF + y * ROWS, 128), ROWS)
        for layer in range(LAYERS):
            product = jnp.dot(
                parts[layer], merged[layer, :, columns], preferred_element_type=F32
            )
            out[i, layer * RANK : layer * RANK + RANK] = (
                product[:RANK] + product[RANK : 2 * RANK] + product[2 * RANK :]
            )
        chosen = jnp.where(wanted == (y * 2 + half) * ROWS, 1.0, 0.0).astype(BF16)
        found = dot_rows(rows, chosen)
        out[i, LEFT:REST] = found[:PART] + found[PART : 2 * PART] + found[2 * PART :]
        out[i, REST:] = rest[...]


def product(own, steps, dest, factor, prepared, merged):
    return pl.pallas_call(
        functools.partial(product_kernel, own, steps),
        in_specs=[whole()] * 5,
        out_specs=whole(),
        out_shape=jax.ShapeDtypeStruct((len(steps), SENT, ROWS), F32),
        compiler_params=params(),
        name="product_own_half" if own else "product_other_half",
    )(dest, factor, *prepared, pltpu.with_memory_space_constraint(merged, pltpu.VMEM))


def add_scaled(pieces):
    scales = [p[REST:, 256:] for p in pieces]
    largest = functools.reduce(jnp.maximum, scales)
    ratios = [scale / largest for scale in scales]
    products = []
    for layer in range(LAYERS):
        ranks = slice(layer * RANK, layer * RANK + RANK)
        terms = []
        for piece, ratio in zip(pieces, ratios):
            row = jnp.broadcast_to(ratio[4 * layer : 4 * layer + 1], (RANK, 128))
            terms.append(piece[ranks] * jnp.concatenate([row] * (ROWS // 128), axis=1))
        products.append(functools.reduce(jnp.add, terms))
    left = functools.reduce(jnp.add, [p[LEFT:REST] for p in pieces])
    gram = functools.reduce(jnp.add, [p[REST:, :256] for p in pieces])
    return products, left, jnp.concatenate([gram, largest], axis=1)


def store_scaled(pieces, out, rest):
    products, left, last = add_scaled(pieces)
    for layer in range(LAYERS):
        out[layer * RANK : layer * RANK + RANK] = products[layer]
    out[LEFT:REST] = left
    rest[...] = last


def pair_kernel(mine, other, *outs):
    for k, out in enumerate(outs):
        store_scaled([mine.at[k], other.at[k]], out, out.at[REST:])


def pair(mine, other):
    return pl.pallas_call(
        pair_kernel,
        in_specs=[whole(), whole()],
        out_specs=[whole()] * len(mine),
        out_shape=[jax.ShapeDtypeStruct((SENT, ROWS), F32)] * len(mine),
        compiler_params=params(),
        name="add_cores",
    )(mine, other)


def line_kernel(a, b, c, d, out, rest):
    store_scaled([a, b, c, d], out, rest)


def line(pieces):
    return pl.pallas_call(
        line_kernel,
        in_specs=[whole()] * YS,
        out_specs=[whole(), whole()],
        out_shape=[
            jax.ShapeDtypeStruct((REST, ROWS), F32),
            jax.ShapeDtypeStruct((SENT - REST, ROWS), F32),
        ],
        compiler_params=params(),
        name="add_line",
    )(*pieces)


def cross_kernel(order, *refs):
    *pieces, out, left = refs
    own, near, far, back = (pieces[order.index(k)] for k in range(XS))
    out[...] = (own[:LEFT] + far[:LEFT]) + (near[:LEFT] + back[:LEFT])
    for k, piece in zip(order, pieces):
        part = lax.rem(lax.axis_index("x") - k + XS, XS)
        left[pl.ds(pl.multiple_of(part * PART, PART), PART)] = piece[LEFT:REST]


def cross(order, pieces):
    return pl.pallas_call(
        functools.partial(cross_kernel, order),
        in_specs=[whole()] * XS,
        out_specs=[whole(), whole()],
        out_shape=[jax.ShapeDtypeStruct((RANKS, ROWS), F32)] * 2,
        compiler_params=params(),
        name="add_cross",
    )(*pieces)


def add_kernel(mate, *refs):
    own, *others, out = refs
    paired = others.pop(mate)
    total = own[...] + paired[...]
    if others:
        total = total + (others[0][...] + others[1][...])
    out[...] = total


def add(mate, *pieces):
    return pl.pallas_call(
        functools.partial(add_kernel, mate),
        in_specs=[whole()] * len(pieces),
        out_specs=whole(),
        out_shape=jax.ShapeDtypeStruct((RANKS, ROWS), F32),
        compiler_params=params(),
        name="add_pieces",
    )(*pieces)


def invert_kernel(rest, rows, out, left_out):
    packed = jnp.concatenate([rest[:, :128], rest[:, 128:256]], axis=0)
    turned = pltpu.roll(packed, 64, 1)
    row = lax.broadcasted_iota(jnp.int32, (RANK, 128), 0)
    lane = lax.broadcasted_iota(jnp.int32, (RANK, 128), 1)
    gram = jnp.concatenate([packed, turned], axis=0)
    unit = jnp.where(row == lax.rem(lane, RANK), 1.0, 0.0)
    work = jnp.where(lane < 64, gram, unit)
    first = lax.rem(lane, 64) < RANK
    for step in range(RANK - 1):
        column = jnp.where(
            first,
            jnp.broadcast_to(work[:, step : step + 1], (RANK, 128)),
            jnp.broadcast_to(work[:, RANK + step : RANK + step + 1], (RANK, 128)),
        )
        pivot = work[step : step + 1] / column[step : step + 1]
        work = work - jnp.where(row > step, column, 0.0) * pivot
    diagonal = [
        jnp.sum(jnp.where(lane == row + l * RANK, work, 0.0), axis=1, keepdims=True)
        for l in range(LAYERS)
    ]
    root = jnp.where(
        first,
        jnp.broadcast_to(diagonal[0], (RANK, 128)),
        jnp.broadcast_to(diagonal[1], (RANK, 128)),
    )
    inverse = pltpu.roll(work / jnp.sqrt(root), 64, 1)
    left = jnp.concatenate(
        [jnp.where(lane < RANK, inverse, 0.0), jnp.where((lane >= RANK) & (lane < 64), inverse, 0.0)],
        axis=0,
    )
    scale = rest[:, 256:]
    out[...] = jnp.concatenate([left[:RANK] * scale[0:1], left[RANK:] * scale[4:5]], axis=0)
    left_out[...] = multiply(left * math.sqrt(COLS), rows[...])


def multiply(triangle, rows):
    return jnp.dot(
        triangle[:, :RANKS], rows, precision=lax.Precision.HIGHEST, preferred_element_type=F32
    )


def invert(rest, rows):
    return pl.pallas_call(
        invert_kernel,
        in_specs=[whole()] * 2,
        out_specs=[whole()] * 2,
        out_shape=[
            jax.ShapeDtypeStruct((RANKS, 128), F32),
            jax.ShapeDtypeStruct((RANKS, ROWS), F32),
        ],
        compiler_params=params(),
        cost_estimate=pl.CostEstimate(flops=2_000_000, bytes_accessed=20_000_000, transcendentals=0),
        name="invert_triangle",
    )(rest, rows)


def apply_kernel(rows, inverse, out):
    out[...] = multiply(inverse, rows[...])


def apply(rows, inverse):
    return pl.pallas_call(
        apply_kernel,
        in_specs=[whole(), whole()],
        out_specs=whole(),
        out_shape=jax.ShapeDtypeStruct((RANKS, ROWS), F32),
        compiler_params=params(),
        name="apply_right",
    )(rows, inverse)


def assemble_kernel(swapped, *refs):
    *pieces, out, sems = refs
    core, at = lax.axis_index("core"), lax.axis_index("y")
    half = 1 - core if swapped else core
    copies = []
    for k, piece in zip(ORDER_LAST, pieces[-YS:]):
        block = lax.rem(at - k + YS, YS)
        columns = pl.ds(pl.multiple_of(half * HALF + block * ROWS, 128), ROWS)
        copies.append(pltpu.make_async_copy(piece, out.at[:, columns], sems.at[k]))
    for copy in copies:
        copy.start()
    for copy in copies:
        copy.wait()


def assemble(pieces, out=None):
    swapped = out is not None
    return pl.pallas_call(
        functools.partial(assemble_kernel, swapped),
        in_specs=[whole(pltpu.HBM)] * swapped + [whole()] * YS,
        out_specs=whole(pltpu.HBM),
        out_shape=jax.ShapeDtypeStruct((RANKS, COLS), F32),
        scratch_shapes=[pltpu.SemaphoreType.DMA((YS,))],
        compiler_params=params(),
        input_output_aliases={0: 0} if swapped else {},
        name="assemble_other_half" if swapped else "assemble_own_half",
    )(*([out] * swapped), *pieces)


def swap(value):
    return lax.ppermute(value, "core", [(0, 1), (1, 0)])


def rotate(value, axis, step):
    size = lax.axis_size(axis)
    return lax.ppermute(value, axis, [(i, (i + step) % size) for i in range(size)])


def along_z(value, even, odd):
    sources = [(z + (odd if z % 2 else even)) % ZS for z in range(ZS)]
    return lax.ppermute(value, "z", [(source, z) for z, source in enumerate(sources)])


def sum_z(value):
    value = add(0, value, along_z(value, 1, -1))
    three, near, two = [along_z(value, at, -at) for at in (-3, -1, 2)]
    return add(0, value, three, near, two)


def turns(values, axis, order):
    return [values[0]] + [rotate(value, axis, k) for value, k in zip(values[1:], order[1:])]


def sum_x(value):
    return add(ORDER_FIRST.index(2) - 1, *turns([value] * XS, "x", ORDER_FIRST))


def shards(gradient, error_buffer, previous_q, run_starts, run_owners):
    q = jnp.swapaxes(previous_q, 1, 2)
    merged, partial, dest = merge(gradient, error_buffer, q, run_starts, run_owners)
    factor = sum_z(sum_x(partial))
    prepared = prepare(factor)
    pieces = {}
    for steps in ((2, 1), (3, 0)):
        sent = swap(product(False, steps, dest, factor, prepared, merged))
        summed = pair(product(True, steps, dest, factor, prepared, merged), sent)
        pieces.update(zip(steps, summed))
    terms, rest = line(turns([pieces[k] for k in ORDER_LINE], "y", ORDER_LINE))
    terms, rows = cross(ORDER_CROSS, turns([terms] * XS, "x", ORDER_CROSS))
    inverse, left = invert(rest, rows)
    right = apply(sum_z(terms), inverse)
    right = turns([right] * YS, "y", ORDER_LAST)
    right = assemble([swap(value) for value in right], assemble(right))
    shape = (LAYERS, RANK, -1)
    return tuple(jnp.swapaxes(value.reshape(shape), 1, 2) for value in (left, right))


def solution(mesh):
    grid = jax.sharding.Mesh(mesh.devices.reshape(XS, ZS, YS, 2), ("x", "z", "y", "core"))
    rep, shard = ("x", "z"), ("y", "core")
    return jax.shard_map(
        shards,
        mesh=grid,
        in_specs=(P(rep, None, shard, None), P(rep, None, shard, None), P(), P(), P()),
        out_specs=(P(None, shard, None), P()),
        check_vma=False,
    )
```

```python
import functools
import math

import jax
import jax.numpy as jnp
from jax import lax
from jax.experimental import pallas as pl
from jax.experimental.pallas import tpu as pltpu
from jax.sharding import PartitionSpec as P

LAYERS = 2
RANK = 32
RANKS = LAYERS * RANK
ROWS = 384
COLS = 3072
HALF = COLS // 2
XS, ZS, YS = 4, 8, 4
PART = RANKS // XS
LEFT, REST = RANKS, RANKS + PART
SENT = REST + 8
CHUNK = 512
CHUNKS = COLS // CHUNK
RUNS = 4
ORDER_FIRST = (0, 2, 3, 1)
ORDER_LINE = (0, 1, 2, 3)
ORDER_CROSS = (0, 2, 3, 1)
ORDER_LAST = (0, 2, 1, 3)
VMEM_LIMIT = 24 * 1024 * 1024
F32 = jnp.float32
BF16 = jnp.bfloat16


def whole(memory_space=pltpu.VMEM):
    return pl.BlockSpec(memory_space=memory_space)


def params(**more):
    return pltpu.CompilerParams(vmem_limit_bytes=VMEM_LIMIT, **more)


def split3(value):
    high = value.astype(BF16)
    rest = value - high.astype(F32)
    middle = rest.astype(BF16)
    low = (rest - middle.astype(F32)).astype(BF16)
    return high, middle, low


def dot_rows(left, right):
    return lax.dot_general(left, right, (((1,), (1,)), ((), ())), preferred_element_type=F32)


def merge_kernel(
    gradient, error, q, starts, owners, merged, partial, dest, g, e, q_in, table, sems, table_sems
):
    tables = [
        pltpu.make_async_copy(source, table.at[i], table_sems.at[i])
        for i, source in enumerate((starts, owners))
    ]
    for copy in tables:
        copy.start()
    copies = []
    for layer in range(LAYERS):
        copies.append([pltpu.make_async_copy(q.at[layer], q_in.at[layer], sems.at[layer, CHUNKS, 0])])
        for chunk in range(CHUNKS):
            columns = pl.ds(chunk * CHUNK, CHUNK)
            copies.append(
                [
                    pltpu.make_async_copy(
                        source.at[0, layer, :, columns],
                        into.at[layer, chunk],
                        sems.at[layer, chunk, i],
                    )
                    for i, (source, into) in enumerate(((gradient, g), (error, e)))
                ]
            )
    for group in copies:
        for copy in group:
            copy.start()
    for copy in tables:
        copy.wait()
    dest[...] = destinations(table)
    arrived = iter(copies)
    for layer in range(LAYERS):
        for copy in next(arrived):
            copy.wait()
        terms = jnp.zeros((RANK, ROWS), F32)
        for chunk in range(CHUNKS):
            for copy in next(arrived):
                copy.wait()
            total = (g[layer, chunk].astype(F32) + e[layer, chunk].astype(F32)).astype(BF16)
            columns = slice(chunk * CHUNK, chunk * CHUNK + CHUNK)
            merged[layer, :, columns] = total
            terms = terms + dot_rows(q_in[layer, :, columns].astype(BF16), total)
        partial[layer * RANK : layer * RANK + RANK] = terms


def destinations(table):
    shard = lax.axis_index("y") * 2 + lax.axis_index("core")
    first = shard * RUNS
    mine = [table[1, first + t] for t in range(RUNS)]

    def count(run, before):
        length = table[0, run + 1] - table[0, run]
        return tuple(b + jnp.where(table[1, run] == o, length, 0) for b, o in zip(before, mine))

    before = lax.fori_loop(0, first, count, (jnp.int32(0),) * RUNS)
    position = shard * ROWS + lax.broadcasted_iota(jnp.int32, (8, ROWS), 1)
    place = position
    for t in range(RUNS):
        start = table[0, first + t]
        moved = position + (mine[t] * ROWS + before[t] - start)
        place = jnp.where(position >= start, moved, place)
    return place


def merge(gradient, error, q, run_starts, run_owners):
    operands = [
        pltpu.with_memory_space_constraint(value, pltpu.HBM)
        for value in (gradient, error, q, run_starts, run_owners)
    ]
    return pl.pallas_call(
        merge_kernel,
        in_specs=[whole(pltpu.HBM)] * 5,
        out_specs=[whole()] * 3,
        out_shape=[
            pltpu.VMEM((LAYERS, ROWS, COLS), BF16),
            jax.ShapeDtypeStruct((RANKS, ROWS), F32),
            jax.ShapeDtypeStruct((8, ROWS), jnp.int32),
        ],
        scratch_shapes=[
            pltpu.VMEM((LAYERS, CHUNKS, ROWS, CHUNK), BF16),
            pltpu.VMEM((LAYERS, CHUNKS, ROWS, CHUNK), BF16),
            pltpu.VMEM((LAYERS, RANK, COLS), F32),
            pltpu.SMEM((2, 2 * YS * RUNS), jnp.int32),
            pltpu.SemaphoreType.DMA((LAYERS, CHUNKS + 1, 2)),
            pltpu.SemaphoreType.DMA((2,)),
        ],
        compiler_params=params(),
        name="merge_project",
    )(*operands)


def prepare_kernel(factor_in, parts, rest):
    factor = factor_in[...]
    biggest = [
        jnp.max(jnp.abs(factor[l * RANK : l * RANK + RANK]), keepdims=True) for l in range(LAYERS)
    ]
    scales = [jnp.where(b > 0, b * 64.0, 1e-30) for b in biggest]
    for layer in range(LAYERS):
        scaled = factor[layer * RANK : layer * RANK + RANK] * (1.0 / scales[layer])
        for i, part in enumerate(split3(scaled)):
            parts[layer, i * RANK : i * RANK + RANK] = part
    high, middle, low = split3(factor)
    left = jnp.concatenate([high, middle, low], axis=0)
    right = jnp.concatenate([high, high, middle, middle, low, low], axis=0)
    gram = dot_rows(left, right)
    gram = gram[:64] + gram[64:128] + gram[128:]
    gram = gram[:, :128] + gram[:, 128:256] + gram[:, 256:]
    lane = lax.broadcasted_iota(jnp.int32, (RANK, 128), 1)
    gram = jnp.where(lax.rem(lane, 64) < 32, gram[:RANK], gram[RANK:])
    gram = jnp.where(lane[:16] < 64, gram[:16], gram[16:])
    scale = jnp.concatenate([jnp.broadcast_to(s, (4, 128)) for s in scales], axis=0)
    rest[...] = jnp.concatenate([gram[:8], gram[8:], scale], axis=1)


def prepare(factor):
    return pl.pallas_call(
        prepare_kernel,
        in_specs=[whole()],
        out_specs=[whole(), whole()],
        out_shape=[
            jax.ShapeDtypeStruct((LAYERS, 3 * RANK, ROWS), BF16),
            jax.ShapeDtypeStruct((8, ROWS), F32),
        ],
        compiler_params=params(),
        name="split_factor",
    )(factor)


def product_kernel(own, steps, dest, factor_in, parts, rest, merged, out):
    half = lax.axis_index("core") if own else 1 - lax.axis_index("core")
    first = pl.multiple_of(lax.axis_index("x") * PART, PART)
    rows = jnp.concatenate(split3(factor_in[pl.ds(first, PART)]), axis=0)
    wanted = jnp.broadcast_to(dest[0:1], (ROWS, ROWS)) - lax.broadcasted_iota(
        jnp.int32, (ROWS, ROWS), 0
    )
    for i, step in enumerate(steps):
        y = lax.rem(lax.axis_index("y") + step, YS)
        columns = pl.ds(pl.multiple_of(half * HALF + y * ROWS, 128), ROWS)
        for layer in range(LAYERS):
            product = jnp.dot(
                parts[layer], merged[layer, :, columns], preferred_element_type=F32
            )
            out[i, layer * RANK : layer * RANK + RANK] = (
                product[:RANK] + product[RANK : 2 * RANK] + product[2 * RANK :]
            )
        chosen = jnp.where(wanted == (y * 2 + half) * ROWS, 1.0, 0.0).astype(BF16)
        found = dot_rows(rows, chosen)
        out[i, LEFT:REST] = found[:PART] + found[PART : 2 * PART] + found[2 * PART :]
        out[i, REST:] = rest[...]


def product(own, steps, dest, factor, prepared, merged):
    return pl.pallas_call(
        functools.partial(product_kernel, own, steps),
        in_specs=[whole()] * 5,
        out_specs=whole(),
        out_shape=jax.ShapeDtypeStruct((len(steps), SENT, ROWS), F32),
        compiler_params=params(),
        name="product_own_half" if own else "product_other_half",
    )(dest, factor, *prepared, pltpu.with_memory_space_constraint(merged, pltpu.VMEM))


def add_scaled(pieces):
    scales = [p[REST:, 256:] for p in pieces]
    largest = functools.reduce(jnp.maximum, scales)
    ratios = [scale / largest for scale in scales]
    products = []
    for layer in range(LAYERS):
        ranks = slice(layer * RANK, layer * RANK + RANK)
        terms = []
        for piece, ratio in zip(pieces, ratios):
            row = jnp.broadcast_to(ratio[4 * layer : 4 * layer + 1], (RANK, 128))
            terms.append(piece[ranks] * jnp.concatenate([row] * (ROWS // 128), axis=1))
        products.append(functools.reduce(jnp.add, terms))
    left = functools.reduce(jnp.add, [p[LEFT:REST] for p in pieces])
    gram = functools.reduce(jnp.add, [p[REST:, :256] for p in pieces])
    return products, left, jnp.concatenate([gram, largest], axis=1)


def store_scaled(pieces, out, rest):
    products, left, last = add_scaled(pieces)
    for layer in range(LAYERS):
        out[layer * RANK : layer * RANK + RANK] = products[layer]
    out[LEFT:REST] = left
    rest[...] = last


def pair_kernel(mine, other, *outs):
    for k, out in enumerate(outs):
        store_scaled([mine.at[k], other.at[k]], out, out.at[REST:])


def pair(mine, other):
    return pl.pallas_call(
        pair_kernel,
        in_specs=[whole(), whole()],
        out_specs=[whole()] * len(mine),
        out_shape=[jax.ShapeDtypeStruct((SENT, ROWS), F32)] * len(mine),
        compiler_params=params(),
        name="add_cores",
    )(mine, other)


def line_kernel(a, b, c, d, out, rest):
    store_scaled([a, b, c, d], out, rest)


def line(pieces):
    return pl.pallas_call(
        line_kernel,
        in_specs=[whole()] * YS,
        out_specs=[whole(), whole()],
        out_shape=[
            jax.ShapeDtypeStruct((REST, ROWS), F32),
            jax.ShapeDtypeStruct((SENT - REST, ROWS), F32),
        ],
        compiler_params=params(),
        name="add_line",
    )(*pieces)


def cross_kernel(order, *refs):
    *pieces, out, left = refs
    own, near, far, back = (pieces[order.index(k)] for k in range(XS))
    out[...] = (own[:LEFT] + far[:LEFT]) + (near[:LEFT] + back[:LEFT])
    for k, piece in zip(order, pieces):
        part = lax.rem(lax.axis_index("x") - k + XS, XS)
        left[pl.ds(pl.multiple_of(part * PART, PART), PART)] = piece[LEFT:REST]


def cross(order, pieces):
    return pl.pallas_call(
        functools.partial(cross_kernel, order),
        in_specs=[whole()] * XS,
        out_specs=[whole(), whole()],
        out_shape=[jax.ShapeDtypeStruct((RANKS, ROWS), F32)] * 2,
        compiler_params=params(),
        name="add_cross",
    )(*pieces)


def add_kernel(mate, *refs):
    own, *others, out = refs
    paired = others.pop(mate)
    total = own[...] + paired[...]
    if others:
        total = total + (others[0][...] + others[1][...])
    out[...] = total


def add(mate, *pieces):
    return pl.pallas_call(
        functools.partial(add_kernel, mate),
        in_specs=[whole()] * len(pieces),
        out_specs=whole(),
        out_shape=jax.ShapeDtypeStruct((RANKS, ROWS), F32),
        compiler_params=params(),
        name="add_pieces",
    )(*pieces)


def invert_kernel(rest, rows, out, left_out):
    packed = jnp.concatenate([rest[:, :128], rest[:, 128:256]], axis=0)
    turned = pltpu.roll(packed, 64, 1)
    row = lax.broadcasted_iota(jnp.int32, (RANK, 128), 0)
    lane = lax.broadcasted_iota(jnp.int32, (RANK, 128), 1)
    gram = jnp.concatenate([packed, turned], axis=0)
    unit = jnp.where(row == lax.rem(lane, RANK), 1.0, 0.0)
    work = jnp.where(lane < 64, gram, unit)
    first = lax.rem(lane, 64) < RANK
    for step in range(RANK - 1):
        column = jnp.where(
            first,
            jnp.broadcast_to(work[:, step : step + 1], (RANK, 128)),
            jnp.broadcast_to(work[:, RANK + step : RANK + step + 1], (RANK, 128)),
        )
        pivot = work[step : step + 1] / column[step : step + 1]
        work = work - jnp.where(row > step, column, 0.0) * pivot
    diagonal = [
        jnp.sum(jnp.where(lane == row + l * RANK, work, 0.0), axis=1, keepdims=True)
        for l in range(LAYERS)
    ]
    root = jnp.where(
        first,
        jnp.broadcast_to(diagonal[0], (RANK, 128)),
        jnp.broadcast_to(diagonal[1], (RANK, 128)),
    )
    inverse = pltpu.roll(work / jnp.sqrt(root), 64, 1)
    left = jnp.concatenate(
        [jnp.where(lane < RANK, inverse, 0.0), jnp.where((lane >= RANK) & (lane < 64), inverse, 0.0)],
        axis=0,
    )
    scale = rest[:, 256:]
    out[...] = jnp.concatenate([left[:RANK] * scale[0:1], left[RANK:] * scale[4:5]], axis=0)
    left_out[...] = multiply(left * math.sqrt(COLS), rows[...])


def multiply(triangle, rows):
    return jnp.dot(
        triangle[:, :RANKS], rows, precision=lax.Precision.HIGHEST, preferred_element_type=F32
    )


def invert(rest, rows):
    return pl.pallas_call(
        invert_kernel,
        in_specs=[whole()] * 2,
        out_specs=[whole()] * 2,
        out_shape=[
            jax.ShapeDtypeStruct((RANKS, 128), F32),
            jax.ShapeDtypeStruct((RANKS, ROWS), F32),
        ],
        compiler_params=params(),
        cost_estimate=pl.CostEstimate(flops=2_000_000, bytes_accessed=20_000_000, transcendentals=0),
        name="invert_triangle",
    )(rest, rows)


def apply_kernel(rows, inverse, out):
    out[...] = multiply(inverse, rows[...])


def apply(rows, inverse):
    return pl.pallas_call(
        apply_kernel,
        in_specs=[whole(), whole()],
        out_specs=whole(),
        out_shape=jax.ShapeDtypeStruct((RANKS, ROWS), F32),
        compiler_params=params(),
        name="apply_right",
    )(rows, inverse)


def assemble_kernel(swapped, *refs):
    *pieces, out, sems = refs
    core, at = lax.axis_index("core"), lax.axis_index("y")
    half = 1 - core if swapped else core
    copies = []
    for k, piece in zip(ORDER_LAST, pieces[-YS:]):
        block = lax.rem(at - k + YS, YS)
        columns = pl.ds(pl.multiple_of(half * HALF + block * ROWS, 128), ROWS)
        copies.append(pltpu.make_async_copy(piece, out.at[:, columns], sems.at[k]))
    for copy in copies:
        copy.start()
    for copy in copies:
        copy.wait()


def assemble(pieces, out=None):
    swapped = out is not None
    return pl.pallas_call(
        functools.partial(assemble_kernel, swapped),
        in_specs=[whole(pltpu.HBM)] * swapped + [whole()] * YS,
        out_specs=whole(pltpu.HBM),
        out_shape=jax.ShapeDtypeStruct((RANKS, COLS), F32),
        scratch_shapes=[pltpu.SemaphoreType.DMA((YS,))],
        compiler_params=params(),
        input_output_aliases={0: 0} if swapped else {},
        name="assemble_other_half" if swapped else "assemble_own_half",
    )(*([out] * swapped), *pieces)


def swap(value):
    return lax.ppermute(value, "core", [(0, 1), (1, 0)])


def rotate(value, axis, step):
    size = lax.axis_size(axis)
    return lax.ppermute(value, axis, [(i, (i + step) % size) for i in range(size)])


def along_z(value, even, odd):
    sources = [(z + (odd if z % 2 else even)) % ZS for z in range(ZS)]
    return lax.ppermute(value, "z", [(source, z) for z, source in enumerate(sources)])


def sum_z(value):
    value = add(0, value, along_z(value, 1, -1))
    three, near, two = [along_z(value, at, -at) for at in (-3, -1, 2)]
    return add(0, value, three, near, two)


def turns(values, axis, order):
    return [values[0]] + [rotate(value, axis, k) for value, k in zip(values[1:], order[1:])]


def sum_x(value):
    return add(ORDER_FIRST.index(2) - 1, *turns([value] * XS, "x", ORDER_FIRST))


def shards(gradient, error_buffer, previous_q, run_starts, run_owners):
    q = jnp.swapaxes(previous_q, 1, 2)
    merged, partial, dest = merge(gradient, error_buffer, q, run_starts, run_owners)
    factor = sum_z(sum_x(partial))
    prepared = prepare(factor)
    pieces = {}
    for steps in ((2, 1), (3, 0)):
        sent = swap(product(False, steps, dest, factor, prepared, merged))
        summed = pair(product(True, steps, dest, factor, prepared, merged), sent)
        pieces.update(zip(steps, summed))
    terms, rest = line(turns([pieces[k] for k in ORDER_LINE], "y", ORDER_LINE))
    terms, rows = cross(ORDER_CROSS, turns([terms] * XS, "x", ORDER_CROSS))
    inverse, left = invert(rest, rows)
    right = apply(sum_z(terms), inverse)
    right = turns([right] * YS, "y", ORDER_LAST)
    right = assemble([swap(value) for value in right], assemble(right))
    shape = (LAYERS, RANK, -1)
    return tuple(jnp.swapaxes(value.reshape(shape), 1, 2) for value in (left, right))


def solution(mesh):
    grid = jax.sharding.Mesh(mesh.devices.reshape(XS, ZS, YS, 2), ("x", "z", "y", "core"))
    rep, shard = ("x", "z"), ("y", "core")
    return jax.shard_map(
        shards,
        mesh=grid,
        in_specs=(P(rep, None, shard, None), P(rep, None, shard, None), P(), P(), P()),
        out_specs=(P(None, shard, None), P()),
        check_vma=False,
    )
```
